256 devices in a mesh: ctx: 32 (over z, y_hi, core), tp: 8 (over x, y_lo).
Axes of the slice: x: 4, y: 4 (y_hi: 2, y_lo: 2; y = y_hi * 2 + y_lo), z: 8, core: 2. Of those that a mesh axis runs over, the one named last changes fastest.
Arguments:
- queries: bfloat16 [2048, 8192], P('ctx', 'tp'), may hold values from -6 to 6
- keys: bfloat16 [32768, 1024], P('ctx', 'tp'), may hold values from -4 to 4
- values: bfloat16 [32768, 1024], P('ctx', 'tp'), may hold values from -6 to 6
- key_segment: int32 [32768], P('ctx'), may hold values from 0 to 7
- key_position: int32 [32768], P('ctx'), may hold values from 0 to 16383, as said below
- query_segment: int32 [2048], P('ctx'), may hold values from 0 to 7, as said below
- query_position: int32 [2048], P('ctx'), may hold values from 1 to 16383, as said below
Outputs:
- attended: bfloat16 [2048, 8192], P('ctx', 'tp')
The draws below stay inside these ranges and needn't reach their ends.
Inputs may be any that keep to these rules, and one draw needn't show every extreme that they name: `key_position`: 8 requests; each request's tokens occupy exactly one key-value slot each, with positions 0 to its length - 1; one request has exactly 16384 tokens and one has exactly 257; the new tokens are the last 256 positions of each request, and their own keys are among the slots; slots and new tokens are assigned to ctx indices in a random order. `query_segment`: request of each new token, 256 tokens each. `query_position`: position of each new token as above.
All inputs are finite; a program needn't handle non-finite values.
Results may differ from the reference program's by a relative error of at most 0.01.
Values may be sent and summed in bfloat16 or wider, within the bound.
No kernel may reach another device: no remote copies, remote signals or barrier semaphores. Data moves between devices by JAX's collectives and lax.ppermute only.
A program may use at most 64 MiB of HBM per device.

```python
import math
import jax
import jax.numpy as jnp
from jax import lax

HEADS = 64
KV_HEADS = 8
HD = 128
CTX_KEYS = 1024
REQS = 8
QUERIES = 2048
KEYS = 32768
N_CTX = 32


def layout(key):
    base = jax.random.fold_in(key, 101)
    key_one, key_two, key_three, key_four = jax.random.split(base, 4)
    per_request = QUERIES // REQS
    longest = jax.random.randint(key_one, (), 0, REQS)
    request_ids = jnp.arange(REQS, dtype=jnp.int32)
    shortest = (longest + 2) % REQS
    weights = jnp.where((request_ids == longest) | (request_ids == shortest), 0, jax.random.randint(key_two, (REQS,), 1, 5)).astype(jnp.int32)
    remaining = KEYS // 2 - (REQS - 1) * (per_request + 1)
    shares = remaining * weights // jnp.sum(weights)
    spare = remaining - jnp.sum(shares)
    shares = shares + jnp.where(request_ids == (longest + 1) % REQS, spare, 0)
    lengths = jnp.where(request_ids == longest, KEYS // 2, per_request + 1 + shares).astype(jnp.int32)
    starts = (jnp.cumsum(lengths) - lengths).astype(jnp.int32)
    order = jax.random.permutation(key_three, KEYS).astype(jnp.int32)
    key_seg = (jnp.sum((order[:, None] >= starts[None, :]).astype(jnp.int32), axis=1) - 1).astype(jnp.int32)
    key_pos = (order - starts[key_seg]).astype(jnp.int32)
    query_order = jax.random.permutation(key_four, QUERIES).astype(jnp.int32)
    query_seg = (query_order // per_request).astype(jnp.int32)
    query_pos = (lengths[query_seg] - per_request + query_order % per_request).astype(jnp.int32)
    return (key_seg, key_pos, query_seg, query_pos)


def draw_key_segment(key, part):
    return layout(key)[0]


def draw_key_position(key, part):
    return layout(key)[1]


def draw_query_segment(key, part):
    return layout(key)[2]


def draw_query_position(key, part):
    return layout(key)[3]


def draw_keys(key, part):
    key = jax.random.fold_in(key, 5)
    drawn = jnp.clip(jax.random.normal(key, (KEYS, KV_HEADS * HD), jnp.float32), -4.0, 4.0)
    return drawn.astype(jnp.bfloat16)


def draw_queries(key, part):
    key = jax.random.fold_in(key, 7)
    drawn = jnp.clip(jax.random.normal(key, (QUERIES, HEADS * HD), jnp.float32), -6.0, 6.0)
    return drawn.astype(jnp.bfloat16)


def shard_levels(stream_key, extent, cuts, least, high):
    def one(dim, blocks):
        heights = jax.random.uniform(jax.random.fold_in(jax.random.fold_in(stream_key, 6), dim), (blocks,), jnp.float32, least / len(cuts), high / len(cuts))
        return jnp.repeat(jnp.exp(heights), extent[dim] // blocks).reshape((-1,) + (1,) * (len(extent) - dim - 1))

    loudness = one(*cuts[0])
    for cut in cuts[1:]:
        loudness = loudness * one(*cut)
    return loudness


def bell_draw(key, dims, width, reach, cuts=(), kind=jnp.bfloat16):
    values = width * jax.random.normal(key, dims, jnp.float32)
    if cuts:
        values = values * shard_levels(key, dims, cuts, -0.22, 0.18)
    return jnp.clip(values, -reach, reach).astype(kind)


def setup_inputs(seed: int = 0) -> dict:
    key_of = jax.random.split(jax.random.key(seed), 8)
    return {
        "queries": draw_queries(jax.random.fold_in(key_of[7], 71), 0),
        "keys": draw_keys(jax.random.fold_in(key_of[7], 71), 0),
        "values": bell_draw(key_of[2], (KEYS, KV_HEADS * HD), 1.0, 6.0, ((0, 32), (1, 8))),
        "key_segment": draw_key_segment(jax.random.fold_in(key_of[7], 71), 0),
        "key_position": draw_key_position(jax.random.fold_in(key_of[7], 71), 0),
        "query_segment": draw_query_segment(jax.random.fold_in(key_of[7], 71), 0),
        "query_position": draw_query_position(jax.random.fold_in(key_of[7], 71), 0),
    }


def block_partial(tile, query_seg, query_pos, block_keys, block_values, key_seg, key_pos):
    rows = tile.shape[0]
    kv_count = block_keys.shape[1]
    head_dim = block_keys.shape[2]
    groups = tile.shape[1] // (kv_count * head_dim)
    query_four = tile.reshape(rows, kv_count, groups, head_dim).astype(jnp.float32)
    scores = jnp.einsum('rkgd,skd->rkgs', query_four, block_keys.astype(jnp.float32)) * (1.0 / math.sqrt(head_dim))
    visible = (query_seg[:, None] == key_seg[None, :]) & (key_pos[None, :] <= query_pos[:, None])
    visible_four = visible[:, None, None, :]
    block_max = lax.optimization_barrier(jnp.max(jnp.where(visible_four, scores, -1e+30), axis=-1))
    expo = jnp.where(visible_four, jnp.exp(scores - block_max[..., None]), 0.0)
    block_total = lax.optimization_barrier(jnp.sum(expo, axis=-1))
    weight = expo.astype(jnp.bfloat16).astype(jnp.float32)
    summed = jnp.einsum('rkgs,skd->rkgd', weight, block_values.astype(jnp.float32))
    block_output = (summed / jnp.maximum(block_total, 1.0)[..., None]).astype(jnp.bfloat16)
    return (block_output.reshape(rows, -1), block_max.reshape(rows, -1), block_total.reshape(rows, -1))

def combine(outputs, maxima, totals):
    count, rows, heads = maxima.shape
    best = lax.optimization_barrier(jnp.max(maxima, axis=0))
    share = totals * jnp.exp(maxima - best[None])
    spread_out = outputs.reshape(count, rows, heads, -1).astype(jnp.float32)
    summed = lax.optimization_barrier(jnp.sum(share[..., None] * spread_out, axis=0))
    return (summed / lax.optimization_barrier(jnp.sum(share, axis=0))[..., None]).astype(jnp.bfloat16).reshape(rows, -1)

def reference(queries, keys, values, key_segment, key_position, query_segment, query_position):
    groups = HEADS // KV_HEADS
    query_heads = queries.reshape(QUERIES, KV_HEADS, groups * HD).transpose(1, 0, 2)
    key_heads = keys.reshape(N_CTX, CTX_KEYS, KV_HEADS, 1, HD).transpose(2, 0, 1, 3, 4)
    value_heads = values.reshape(N_CTX, CTX_KEYS, KV_HEADS, 1, HD).transpose(2, 0, 1, 3, 4)
    seg_blocks = key_segment.reshape(N_CTX, CTX_KEYS)
    pos_blocks = key_position.reshape(N_CTX, CTX_KEYS)

    def one_head(operands):
        query_one, key_one, value_one = operands

        def one_block(pieces):
            block_keys, block_values, block_seg, block_pos = pieces
            return block_partial(query_one, query_segment, query_position, block_keys, block_values, block_seg, block_pos)
        outputs, maxima, totals = lax.map(one_block, (key_one, value_one, seg_blocks, pos_blocks))
        return combine(outputs, maxima, totals)
    result = lax.map(one_head, (query_heads, key_heads, value_heads))
    return result.transpose(1, 0, 2).reshape(QUERIES, HEADS * HD)
```

```python
import functools
import math

import jax
import jax.numpy as jnp
from jax import lax
from jax.experimental import pallas as pl
from jax.experimental.pallas import tpu as pltpu
from jax.sharding import PartitionSpec as P

HD = 128
LANES = 128
REQS = 8
SPAN = 16384
BIG = 1e9
NEG = -1e30
SCALE2 = math.log2(math.e) / math.sqrt(HD)
LN2 = math.log(2.0)
PLANE = 4
PIECE = 64
CHUNK = 512
GROUP = 80
VMEM_BYTES = 48 * 1024 * 1024
F32 = jnp.float32
BF16 = jnp.bfloat16

NT = (((1,), (1,)), ((), ()))


def iota(shape, dim):
    return lax.broadcasted_iota(jnp.int32, shape, dim)


def pack_kernel(q_ref, k_ref, v_ref, kseg_ref, kpos_ref, qseg_ref, qpos_ref, kv_ref, qp_ref):
    slots = k_ref.shape[0]
    tiles = slots // LANES
    tokens = q_ref.shape[0]
    width = q_ref.shape[1]
    copies = qp_ref.shape[0]

    qseg = qseg_ref[...].astype(F32)
    qhi = (qpos_ref[...] >> 7).astype(F32)
    qlo = (qpos_ref[...] & 127).astype(F32)
    rows = jnp.concatenate([qseg, qhi, qlo, jnp.zeros((LANES - 3, tokens), F32)], axis=0)
    labels = jnp.transpose(rows).astype(BF16)
    for n in range(copies):
        qp_ref[n, :, :width] = q_ref[...]
        qp_ref[n, :, width:] = labels

    seg = kseg_ref[...]
    pos = kpos_ref[...]
    code = (seg * SPAN + pos).astype(F32)
    ranks = [jnp.zeros((1, LANES), F32) for _ in range(tiles)]
    for t in range(tiles):
        col = jnp.transpose(jnp.broadcast_to(code[t : t + 1, :], (LANES, LANES)))
        for u in range(tiles):
            less = jnp.where(col < code[u : u + 1, :], 1.0, 0.0)
            ranks[u] = ranks[u] + jnp.sum(less, axis=0, keepdims=True)
    rank = jnp.concatenate(ranks, axis=1).astype(jnp.int32)
    place = jnp.where(iota((slots, slots), 0) == rank, 1.0, 0.0).astype(BF16)
    kv_ref[0:slots, :] = jnp.dot(place, k_ref[...], preferred_element_type=F32).astype(BF16)
    kv_ref[slots : 2 * slots, :] = jnp.dot(place, v_ref[...], preferred_element_type=F32).astype(BF16)
    flat = lambda x: jnp.concatenate([x[t : t + 1, :] for t in range(tiles)], axis=1)
    labs = jnp.concatenate(
        [flat(seg.astype(F32)), flat((pos >> 7).astype(F32)), flat((pos & 127).astype(F32)),
         jnp.zeros((5, slots), F32)], axis=0)
    moved = lax.dot_general(labs.astype(BF16), place, NT, preferred_element_type=F32)
    parts = [moved[w : w + 1, t * LANES : (t + 1) * LANES] for w in range(3) for t in range(tiles)]
    parts.append(jnp.zeros((32 - 3 * tiles, LANES), F32))
    kv_ref[2 * slots :, :] = jnp.concatenate(parts, axis=0).astype(BF16)


def gather_kernel(*refs):
    blocks = refs[:PLANE]
    kc_ref, vc_ref, kk_ref, meta_ref, norm_ref, shifted_ref, start_vmem, start_smem, sem = refs[PLANE:]
    slots = (blocks[0].shape[0] - 32) // 2
    tiles = slots // LANES
    lane = iota((tiles, LANES), 1)
    lane1 = iota((1, LANES), 1)
    ones = jnp.ones((HD, LANES), BF16)
    best = jnp.zeros((1, 1), F32)
    table = jnp.zeros((16, LANES), F32)
    for b in range(PLANE):
        ref = blocks[b]
        lab = ref[2 * slots : 2 * slots + 32, :].astype(F32)
        code = lab[:tiles] * SPAN + lab[tiles : 2 * tiles] * 128.0 + lab[2 * tiles : 3 * tiles]
        after = jnp.concatenate([code[1:], code[:1]], axis=0)
        for s in range(8):
            step = 16 * s
            if s == 0:
                shifted_ref[b * 8] = code
            else:
                shifted_ref[b * 8 + s] = jnp.where(
                    lane < LANES - step,
                    pltpu.roll(code, LANES - step, 1),
                    pltpu.roll(after, LANES - step, 1),
                )
        below = [
            jnp.sum(jnp.where(code < float(r * SPAN), 1.0, 0.0), axis=0, keepdims=True)
            for r in range(REQS + 1)
        ]
        below.append(jnp.zeros((16 - REQS - 1, LANES), F32))
        counts = jnp.sum(jnp.concatenate(below, axis=0), axis=1, keepdims=True)
        table = jnp.where(iota((16, LANES), 1) == b, counts, table)
        k = ref[0:slots, :]
        sums = jnp.dot(k * k, ones, preferred_element_type=F32)
        best = jnp.maximum(best, jnp.max(sums, axis=(0, 1), keepdims=True))
    norm_ref[...] = jnp.broadcast_to(best, norm_ref.shape)
    start_vmem[...] = table.astype(jnp.int32)
    copy = pltpu.make_async_copy(start_vmem, start_smem, sem)
    copy.start()
    copy.wait()

    per_chunk = CHUNK // PIECE
    zeros = jnp.zeros((PIECE, HD), BF16)

    def request(r, piece):
        meta_ref[0, r] = piece // per_chunk
        first = (r * SPAN).astype(F32)
        for b in range(PLANE):
            lo = start_smem[r, b]
            hi = start_smem[r + 1, b]
            base = lo & ~15
            count = jnp.where(hi > lo, (hi - base + PIECE - 1) // PIECE, 0)

            def one(j, held, b=b, base=base, first=first):
                want = base + j * PIECE
                have = pl.multiple_of(jnp.minimum(want, slots - PIECE), 16)
                dest = pl.multiple_of(held * PIECE, PIECE)
                kc_ref[pl.ds(dest, PIECE), :] = blocks[b][pl.ds(have, PIECE), :]
                vc_ref[pl.ds(dest, PIECE), :] = blocks[b][pl.ds(slots + have, PIECE), :]
                row = shifted_ref[b * 8 + (have % LANES) // 16, pl.ds(have // LANES, 1), :]
                good = (row >= first) & (row < first + SPAN) & (lane1 + have >= want)
                kk_ref[pl.ds(held, 1), :] = jnp.where(good, row, BIG)
                return held + 1

            piece = lax.fori_loop(0, count, one, piece)

        def fill(j, held):
            dest = pl.multiple_of(held * PIECE, PIECE)
            kc_ref[pl.ds(dest, PIECE), :] = zeros
            vc_ref[pl.ds(dest, PIECE), :] = zeros
            kk_ref[pl.ds(held, 1), :] = jnp.full((1, LANES), BIG, F32)
            return held + 1

        rest = (-piece) % per_chunk
        piece = lax.fori_loop(0, rest, fill, piece)
        meta_ref[1, r] = piece // per_chunk
        return piece

    lax.fori_loop(0, REQS, request, jnp.int32(0))


def attend_kernel(
    q_ref, kc_ref, vc_ref, kk_ref, meta_ref, norm_ref, o_ref,
    qs_ref, qcode_ref, os_ref, qg_ref, acc_ref, total_ref, top_ref, span_ref,
):
    tokens = q_ref.shape[0]
    heads = (q_ref.shape[1] - LANES) // HD
    width = heads * HD
    padded = tokens + REQS * 16
    rows = heads * GROUP

    lab = q_ref[:, width:].astype(F32)
    lab_t = jnp.transpose(lab)
    seg_row = lab_t[0:1]
    code_row = seg_row * SPAN + lab_t[1:2] * 128.0 + lab_t[2:3]
    seg_col = lab[:, 0:1]
    code_col = seg_col * SPAN + lab[:, 1:2] * 128.0 + lab[:, 2:3]
    rank_row = jnp.sum(jnp.where(code_col < code_row, 1.0, 0.0), axis=0, keepdims=True)
    rank_col = jnp.sum(jnp.where(code_row < code_col, 1.0, 0.0), axis=1, keepdims=True)
    used = jnp.int32(0)
    plain = jnp.int32(0)
    for r in range(REQS):
        count = jnp.sum(jnp.where(seg_row == float(r), 1.0, 0.0)).astype(jnp.int32)
        span_ref[0, r] = used
        span_ref[1, r] = count
        extra = (used - plain).astype(F32)
        rank_row = rank_row + jnp.where(seg_row == float(r), extra, 0.0)
        rank_col = rank_col + jnp.where(seg_col == float(r), extra, 0.0)
        used = used + ((count + 15) // 16) * 16
        plain = plain + count
    place = jnp.where(
        iota((padded, tokens), 0) == rank_row.astype(jnp.int32), 1.0, 0.0
    ).astype(BF16)
    back = jnp.where(
        iota((tokens, padded), 1) == rank_col.astype(jnp.int32), 1.0, 0.0
    ).astype(BF16)
    for h in range(heads):
        qs_ref[h, 0:padded, :] = jnp.dot(
            place, q_ref[:, h * HD : (h + 1) * HD], preferred_element_type=F32
        ).astype(BF16)
        qs_ref[h, padded:, :] = jnp.zeros((GROUP, HD), BF16)
    lab_s = jnp.dot(place, q_ref[:, width:], preferred_element_type=F32)
    qcode = lab_s[:, 0:1] * SPAN + lab_s[:, 1:2] * 128.0 + lab_s[:, 2:3]
    qcode_ref[0:padded, :] = jnp.broadcast_to(qcode, (padded, LANES))
    qcode_ref[padded:, :] = jnp.zeros((GROUP, LANES), F32)
    os_ref[...] = jnp.zeros(os_ref.shape, BF16)

    q_sums = jnp.zeros((tokens, LANES), F32)
    ones = jnp.ones((HD, LANES), BF16)
    for h in range(heads):
        q = q_ref[:, h * HD : (h + 1) * HD]
        q_sums = jnp.maximum(q_sums, jnp.dot(q * q, ones, preferred_element_type=F32))
    bound = jnp.max(q_sums) * jnp.max(norm_ref[...]) * (1.05 * SCALE2 * SCALE2)
    large = bound > 80.0 * 80.0

    lane = iota((1, LANES), 1)
    parts = CHUNK // LANES

    def slot_codes(c):
        held = kk_ref[pl.ds(pl.multiple_of(c * (CHUNK // PIECE), 8), 8), :]
        return [
            jnp.where(
                lane < PIECE,
                held[2 * n : 2 * n + 1],
                pltpu.roll(held[2 * n + 1 : 2 * n + 2], PIECE, 1),
            )
            for n in range(parts)
        ]

    def scores_of(c):
        k = kc_ref[pl.ds(pl.multiple_of(c * CHUNK, CHUNK), CHUNK), :]
        return lax.dot_general(qg_ref[...], k, NT, preferred_element_type=F32) * SCALE2

    def request(r, carry):
        first = span_ref[0, r]
        count = span_ref[1, r]
        chunk_lo = meta_ref[0, r]
        chunk_hi = meta_ref[1, r]

        def group(g, carry):
            row0 = pl.multiple_of(first + g * GROUP, 16)
            for h in range(heads):
                qg_ref[h * GROUP : (h + 1) * GROUP, :] = qs_ref[h, pl.ds(row0, GROUP), :]
            limit = qcode_ref[pl.ds(row0, GROUP), :]
            acc_ref[...] = jnp.zeros((rows, HD), F32)
            total_ref[...] = jnp.zeros((rows, LANES), F32)
            top_ref[...] = jnp.zeros((rows, LANES), F32)

            @pl.when(large)
            def _():
                top_ref[...] = jnp.full((rows, LANES), NEG, F32)

                def look(c, carry):
                    codes = slot_codes(c)
                    s = scores_of(c)
                    for n in range(parts):
                        mask = codes[n] <= limit
                        for h in range(heads):
                            at = slice(h * GROUP, (h + 1) * GROUP)
                            part = jnp.where(mask, s[at, n * LANES : (n + 1) * LANES], NEG)
                            top_ref[at, :] = jnp.maximum(top_ref[at, :], part)
                    return carry

                lax.fori_loop(chunk_lo, chunk_hi, look, 0)
                best = jnp.max(top_ref[...], axis=1, keepdims=True)
                top_ref[...] = jnp.broadcast_to(jnp.where(best < 0.5 * NEG, 0.0, best), (rows, LANES))

            def step(c, carry):
                codes = slot_codes(c)
                s = scores_of(c)
                weights = []
                for n in range(parts):
                    mask = codes[n] <= limit
                    column = []
                    for h in range(heads):
                        at = slice(h * GROUP, (h + 1) * GROUP)
                        part = s[at, n * LANES : (n + 1) * LANES] - top_ref[at, :]
                        e = jnp.exp2(jnp.where(mask, part, NEG))
                        total_ref[at, :] += e
                        column.append(e.astype(BF16))
                    weights.append(jnp.concatenate(column, axis=0))
                v = vc_ref[pl.ds(pl.multiple_of(c * CHUNK, CHUNK), CHUNK), :]
                acc_ref[...] += jnp.dot(
                    jnp.concatenate(weights, axis=1), v, preferred_element_type=F32
                )
                return carry

            lax.fori_loop(chunk_lo, chunk_hi, step, 0)

            total = jnp.sum(total_ref[...], axis=1, keepdims=True)
            some = total > 0.0
            safe = jnp.where(some, total, 1.0)
            out = acc_ref[...] * (1.0 / safe)
            share = jnp.where(some, top_ref[:, 0:1] + jnp.log2(safe), NEG)
            block = jnp.zeros((GROUP, LANES), F32)
            wide = iota((GROUP, LANES), 1)
            for h in range(heads):
                at = slice(h * GROUP, (h + 1) * GROUP)
                os_ref[pl.ds(row0, GROUP), h * HD : (h + 1) * HD] = out[at].astype(BF16)
                one = share[at]
                high = one.astype(BF16).astype(F32)
                middle = (one - high).astype(BF16).astype(F32)
                low = one - high - middle
                block = jnp.where(wide == h, high, block)
                block = jnp.where(wide == heads + h, middle, block)
                block = jnp.where(wide == 2 * heads + h, low, block)
            os_ref[pl.ds(row0, GROUP), width:] = block.astype(BF16)
            return carry

        lax.fori_loop(0, (count + GROUP - 1) // GROUP, group, 0)
        return carry

    lax.fori_loop(0, REQS, request, 0)
    o_ref[...] = jnp.dot(back, os_ref[0:padded, :], preferred_element_type=F32).astype(BF16)


def combine_kernel(parts_ref, o_ref):
    count = parts_ref.shape[0]
    heads = o_ref.shape[1] // HD
    width = heads * HD
    shares = []
    for n in range(count):
        lab = parts_ref[n, :, width:].astype(F32)
        shares.append(lab + pltpu.roll(lab, LANES - heads, 1) + pltpu.roll(lab, LANES - 2 * heads, 1))
    best = functools.reduce(jnp.maximum, shares)
    weights = [jnp.exp2(s - best) for s in shares]
    scale = 1.0 / sum(weights)
    weights = [w * scale for w in weights]
    for h in range(heads):
        at = slice(h * HD, (h + 1) * HD)
        acc = weights[0][:, h : h + 1] * parts_ref[0, :, at].astype(F32)
        for n in range(1, count):
            acc = acc + weights[n][:, h : h + 1] * parts_ref[n, :, at].astype(F32)
        o_ref[:, at] = acc.astype(BF16)


def params():
    return pltpu.CompilerParams(vmem_limit_bytes=VMEM_BYTES)


def on_device(queries, keys, values, key_segment, key_position, query_segment, query_position):
    cycle = lax.axis_size("ctx")
    planes = cycle // PLANE
    tokens, width = queries.shape
    slots = keys.shape[0]
    wide = width + LANES
    kv, qp = pl.pallas_call(
        pack_kernel,
        out_shape=(
            jax.ShapeDtypeStruct((2 * slots + 32, HD), BF16),
            jax.ShapeDtypeStruct((planes, tokens, wide), BF16),
        ),
        compiler_params=params(),
        name="pack",
    )(
        queries, keys, values,
        key_segment.reshape(slots // LANES, LANES), key_position.reshape(slots // LANES, LANES),
        query_segment.reshape(1, tokens), query_position.reshape(1, tokens),
    )

    def swapped(x, bits):
        return lax.ppermute(x, "ctx", [(i, i ^ bits) for i in range(cycle)])

    kv_y = swapped(kv, 2)
    kv_c = swapped(kv, 1)
    kv_yc = swapped(kv_y, 1)
    along = [[PLANE * z + j for z in range(planes)] for j in range(PLANE)]
    q_all = lax.all_to_all(qp, "ctx", 0, 0, tiled=True, axis_index_groups=along)

    pieces = (PLANE * slots + PLANE * REQS * 15) // PIECE + PLANE * REQS
    chunks = (pieces + REQS * (CHUNK // PIECE - 1)) // (CHUNK // PIECE) + 1
    smem = pl.BlockSpec(memory_space=pltpu.SMEM)
    vmem = pl.BlockSpec(memory_space=pltpu.VMEM)
    kc, vc, kk, meta, norm = pl.pallas_call(
        gather_kernel,
        out_shape=(
            jax.ShapeDtypeStruct((chunks * CHUNK, HD), BF16),
            jax.ShapeDtypeStruct((chunks * CHUNK, HD), BF16),
            jax.ShapeDtypeStruct((chunks * (CHUNK // PIECE), LANES), F32),
            jax.ShapeDtypeStruct((2, REQS), jnp.int32),
            jax.ShapeDtypeStruct((8, LANES), F32),
        ),
        out_specs=(vmem, vmem, vmem, smem, vmem),
        scratch_shapes=[
            pltpu.VMEM((PLANE * 8, slots // LANES, LANES), F32),
            pltpu.VMEM((16, LANES), jnp.int32),
            pltpu.SMEM((16, LANES), jnp.int32),
            pltpu.SemaphoreType.DMA,
        ],
        compiler_params=params(),
        name="gather",
    )(kv, kv_c, kv_y, kv_yc)

    everyone = planes * tokens
    heads = width // HD
    padded = everyone + REQS * 16 + GROUP
    rows = heads * GROUP
    parts = pl.pallas_call(
        attend_kernel,
        out_shape=jax.ShapeDtypeStruct((everyone, wide), BF16),
        in_specs=[vmem, vmem, vmem, vmem, smem, vmem],
        scratch_shapes=[
            pltpu.VMEM((heads, padded, HD), BF16),
            pltpu.VMEM((padded, LANES), F32),
            pltpu.VMEM((padded, wide), BF16),
            pltpu.VMEM((rows, HD), BF16),
            pltpu.VMEM((rows, HD), F32),
            pltpu.VMEM((rows, LANES), F32),
            pltpu.VMEM((rows, LANES), F32),
            pltpu.SMEM((2, REQS), jnp.int32),
        ],
        compiler_params=params(),
        name="attend",
    )(q_all.reshape(everyone, wide), kc, vc, kk, meta, norm)

    got = lax.all_to_all(
        parts.reshape(planes, tokens, wide), "ctx", 0, 0, tiled=True, axis_index_groups=along
    )
    return pl.pallas_call(
        combine_kernel,
        out_shape=jax.ShapeDtypeStruct((tokens, width), BF16),
        compiler_params=params(),
        name="combine",
    )(got)


def solution(mesh):
    placed = (
        P("ctx", "tp"),
        P("ctx", "tp"),
        P("ctx", "tp"),
        P("ctx"),
        P("ctx"),
        P("ctx"),
        P("ctx"),
    )
    return jax.shard_map(
        on_device, mesh=mesh, in_specs=placed, out_specs=P("ctx", "tp"), check_vma=False
    )
```

```python
import functools
import math

import jax
import jax.numpy as jnp
from jax import lax
from jax.experimental import pallas as pl
from jax.experimental.pallas import tpu as pltpu
from jax.sharding import PartitionSpec as P

HD = 128
LANES = 128
REQS = 8
SPAN = 16384
BIG = 1e9
NEG = -1e30
SCALE2 = math.log2(math.e) / math.sqrt(HD)
LN2 = math.log(2.0)
PLANE = 4
CHUNK = PLANE * LANES
NEAR_GROUP = 48
FAR_GROUP = 32
VMEM_BYTES = 32 * 1024 * 1024
ALL_VMEM = 62 * 1024 * 1024
F32 = jnp.float32
BF16 = jnp.bfloat16

NT = (((1,), (1,)), ((), ()))


def iota(shape, dim):
    return lax.broadcasted_iota(jnp.int32, shape, dim)


def pack_kernel(*refs):
    far, (kv_ref, qp_ref), near, sems = refs[:7], refs[7:9], refs[9:16], refs[16]
    copies = [pltpu.make_async_copy(a, b, sems.at[n]) for n, (a, b) in enumerate(zip(far, near))]
    for copy in copies:
        copy.start()
    for copy in copies:
        copy.wait()
    q_ref, k_ref, v_ref, kseg_ref, kpos_ref, qseg_ref, qpos_ref = near
    slots = k_ref.shape[0]
    tiles = slots // LANES
    tokens = q_ref.shape[0]
    width = q_ref.shape[1]

    qseg = qseg_ref[...].astype(F32)
    qhi = (qpos_ref[...] >> 7).astype(F32)
    qlo = (qpos_ref[...] & 127).astype(F32)
    rows = jnp.concatenate([qseg, qhi, qlo, jnp.zeros((LANES - 3, tokens), F32)], axis=0)
    labels = jnp.transpose(rows).astype(BF16)
    qp_ref[:, :width] = q_ref[...]
    qp_ref[:, width:] = labels

    seg = kseg_ref[...]
    pos = kpos_ref[...]
    code = (seg * SPAN + pos).astype(F32)
    ranks = [jnp.zeros((1, LANES), F32) for _ in range(tiles)]
    for t in range(tiles):
        col = jnp.transpose(jnp.broadcast_to(code[t : t + 1, :], (LANES, LANES)))
        for u in range(tiles):
            less = jnp.where(col < code[u : u + 1, :], 1.0, 0.0)
            ranks[u] = ranks[u] + jnp.sum(less, axis=0, keepdims=True)
    rank = jnp.concatenate(ranks, axis=1).astype(jnp.int32)
    place = jnp.where(iota((slots, slots), 0) == rank, 1.0, 0.0).astype(BF16)
    kv_ref[0:slots, :] = jnp.dot(place, k_ref[...], preferred_element_type=F32).astype(BF16)
    kv_ref[slots : 2 * slots, :] = jnp.dot(place, v_ref[...], preferred_element_type=F32).astype(BF16)
    flat = lambda x: jnp.concatenate([x[t : t + 1, :] for t in range(tiles)], axis=1)
    labs = jnp.concatenate(
        [flat(seg.astype(F32)), flat((pos >> 7).astype(F32)), flat((pos & 127).astype(F32)),
         jnp.zeros((5, slots), F32)], axis=0)
    moved = lax.dot_general(labs.astype(BF16), place, NT, preferred_element_type=F32)
    parts = [moved[w : w + 1, t * LANES : (t + 1) * LANES] for w in range(3) for t in range(tiles)]
    k = k_ref[...]
    sums = jnp.dot(k * k, jnp.ones((HD, LANES), BF16), preferred_element_type=F32)
    parts.append(jnp.max(sums, axis=0, keepdims=True) * 1.02)
    parts.append(jnp.zeros((31 - 3 * tiles, LANES), F32))
    kv_ref[2 * slots :, :] = jnp.concatenate(parts, axis=0).astype(BF16)


def table_kernel(*refs):
    blocks = refs[:PLANE]
    kk_ref, from_ref, meta_ref, norm_ref, shifted_ref, start_vmem, start_smem, sem = refs[PLANE:]
    slots = (blocks[0].shape[0] - 32) // 2
    tiles = slots // LANES
    lane = iota((tiles, LANES), 1)
    lane1 = iota((1, LANES), 1)
    best = jnp.zeros((1, LANES), F32)
    table = jnp.zeros((16, LANES), F32)
    for b in range(PLANE):
        lab = blocks[b][2 * slots : 2 * slots + 32, :].astype(F32)
        code = lab[:tiles] * SPAN + lab[tiles : 2 * tiles] * 128.0 + lab[2 * tiles : 3 * tiles]
        best = jnp.maximum(best, lab[3 * tiles : 3 * tiles + 1])
        below = [
            jnp.sum(jnp.where(code < float(r * SPAN), 1.0, 0.0), axis=0, keepdims=True)
            for r in range(REQS + 1)
        ]
        below.append(jnp.zeros((16 - REQS - 1, LANES), F32))
        counts = jnp.sum(jnp.concatenate(below, axis=0), axis=1, keepdims=True)
        table = jnp.where(iota((16, LANES), 1) == b, counts, table)
    start_vmem[...] = table.astype(jnp.int32)
    copy = pltpu.make_async_copy(start_vmem, start_smem, sem)
    copy.start()
    norm_ref[...] = jnp.broadcast_to(best, norm_ref.shape)
    for b in range(PLANE):
        lab = blocks[b][2 * slots : 2 * slots + 32, :].astype(F32)
        code = lab[:tiles] * SPAN + lab[tiles : 2 * tiles] * 128.0 + lab[2 * tiles : 3 * tiles]
        after = jnp.concatenate([code[1:], code[:1]], axis=0)
        shifted_ref[b * 8] = code
        for n in range(1, 8):
            step = 16 * n
            shifted_ref[b * 8 + n] = jnp.where(
                lane < LANES - step,
                pltpu.roll(code, LANES - step, 1),
                pltpu.roll(after, LANES - step, 1),
            )
    copy.wait()

    def request(r, made):
        first = (r * SPAN).astype(F32)
        bases = []
        count = jnp.int32(0)
        for b in range(PLANE):
            lo = start_smem[r, b]
            hi = start_smem[r + 1, b]
            base = lo & ~15
            bases.append(base)
            count = jnp.maximum(count, jnp.where(hi > lo, (hi - base + LANES - 1) // LANES, 0))

        def one(j, carry):
            for b in range(PLANE):
                want = bases[b] + j * LANES
                have = jnp.minimum(want, slots - LANES)
                from_ref[b, made + j] = have
                row = shifted_ref[b * 8 + (have % LANES) // 16, pl.ds(have // LANES, 1), :]
                good = (row >= first) & (row < first + SPAN) & (lane1 + have >= want)
                kk_ref[pl.ds((made + j) * PLANE + b, 1), :] = jnp.where(good, row, BIG)
            return carry

        lax.fori_loop(0, count, one, 0)
        meta_ref[0, r] = made
        meta_ref[1, r] = made + count
        return made + count

    lax.fori_loop(0, REQS, request, jnp.int32(0))


def order_kernel(group, *refs):
    q_refs, (qs_ref, qcode_ref, back_ref, span_ref, norm_ref, q_ref) = refs[:-6], refs[-6:]
    each = q_refs[0].shape[0]
    for n, ref in enumerate(q_refs):
        q_ref[n * each : (n + 1) * each, :] = ref[...]
    tokens = q_ref.shape[0]
    heads = qs_ref.shape[0]
    width = heads * HD
    padded = tokens + REQS * 16
    lab = q_ref[:, width:].astype(F32)
    lab_t = jnp.transpose(lab)
    seg_row = lab_t[0:1]
    code_row = seg_row * SPAN + lab_t[1:2] * 128.0 + lab_t[2:3]
    seg_col = lab[:, 0:1]
    code_col = seg_col * SPAN + lab[:, 1:2] * 128.0 + lab[:, 2:3]
    rank_row = jnp.sum(jnp.where(code_col < code_row, 1.0, 0.0), axis=0, keepdims=True)
    rank_col = jnp.sum(jnp.where(code_row < code_col, 1.0, 0.0), axis=1, keepdims=True)
    counts = [
        jnp.sum(jnp.where(seg_row == float(r), 1.0, 0.0), axis=1, keepdims=True) for r in range(REQS)
    ]
    extra = jnp.zeros((1, 1), F32)
    for r in range(REQS):
        rank_row = rank_row + jnp.where(seg_row == float(r), extra, 0.0)
        rank_col = rank_col + jnp.where(seg_col == float(r), extra, 0.0)
        extra = extra + (jnp.ceil(counts[r] * (1.0 / 16.0)) * 16.0 - counts[r])
    used = jnp.int32(0)
    for r in range(REQS):
        count = jnp.max(counts[r]).astype(jnp.int32)
        span_ref[0, r] = used
        span_ref[1, r] = (count + group - 1) // group
        used = used + ((count + 15) // 16) * 16
    place = jnp.where(
        iota((padded, tokens), 0) == rank_row.astype(jnp.int32), 1.0, 0.0
    ).astype(BF16)
    back_ref[...] = jnp.where(
        iota((tokens, padded), 1) == rank_col.astype(jnp.int32), 1.0, 0.0
    ).astype(BF16)
    ones = jnp.ones((HD, LANES), BF16)
    sums = jnp.zeros((padded, LANES), F32)
    for h in range(heads):
        q = jnp.dot(place, q_ref[:, h * HD : (h + 1) * HD], preferred_element_type=F32)
        q = (q * SCALE2).astype(BF16)
        qs_ref[h, 0:padded, :] = q
        qs_ref[h, padded:, :] = jnp.zeros((group, HD), BF16)
        sums = jnp.maximum(sums, jnp.dot(q * q, ones, preferred_element_type=F32))
    norm_ref[...] = jnp.broadcast_to(jnp.max(sums, axis=0, keepdims=True), norm_ref.shape)
    lab_s = jnp.dot(place, q_ref[:, width:], preferred_element_type=F32)
    qcode = lab_s[:, 0:1] * SPAN + lab_s[:, 1:2] * 128.0 + lab_s[:, 2:3]
    qcode_ref[0:padded, :] = jnp.broadcast_to(qcode, (padded, LANES))
    qcode_ref[padded:, :] = jnp.zeros((group, LANES), F32)


def attend_kernel(group, *refs):
    qs_ref, qcode_ref, back_ref, span_ref, qnorm_ref = refs[:5]
    blocks, (kk_ref, from_ref, meta_ref, norm_ref, _) = refs[5:9], refs[9:14]
    o_refs = refs[14:-8]
    os_ref, acc_ref, total_ref, top_ref, shift_ref, score_a, score_b, steps_ref = refs[-8:]
    heads = qs_ref.shape[0]
    width = heads * HD
    tokens, padded = back_ref.shape
    each = o_refs[0].shape[0]

    made = jnp.int32(0)
    for r in range(REQS):
        chunk_lo = meta_ref[0, r]
        chunk_hi = meta_ref[1, r]

        def one_group(g, made, r=r, chunk_lo=chunk_lo, chunk_hi=chunk_hi):
            def one_chunk(c, made):
                steps_ref[0, made] = span_ref[0, r] + g * group
                steps_ref[1, made] = c
                steps_ref[2, made] = r * SPAN
                return made + 1

            return lax.fori_loop(chunk_lo, chunk_hi, one_chunk, made)

        made = lax.fori_loop(0, span_ref[1, r], one_group, made)
    for n in range(3):
        steps_ref[0, made + n] = 0
        steps_ref[1, made + n] = 0
        steps_ref[2, made + n] = REQS * SPAN
    acc_ref[...] = jnp.zeros(acc_ref.shape, F32)
    total_ref[...] = jnp.zeros(total_ref.shape, F32)

    large = jnp.max(qnorm_ref[...] * norm_ref[...]) * 1.05 > 80.0 * 80.0

    slots = (blocks[0].shape[0] - 32) // 2
    ones = jnp.ones((CHUNK, LANES), BF16)

    def masks(s):
        row0 = pl.multiple_of(steps_ref[0, s], 16)
        first = steps_ref[2, s].astype(F32)
        code = qcode_ref[pl.ds(row0, group), :]
        limit = jnp.where((code >= first) & (code < first + SPAN), code, -1.0)
        row = steps_ref[1, s] * PLANE
        return [kk_ref[pl.ds(row + b, 1), :] <= limit for b in range(PLANE)]

    def slots_of(s, base):
        c = steps_ref[1, s]
        return jnp.concatenate(
            [
                blocks[b][pl.ds(pl.multiple_of(base + from_ref[b, c], 16), LANES), :]
                for b in range(PLANE)
            ],
            axis=0,
        )

    def rows_of(s, h):
        return h, pl.ds(pl.multiple_of(steps_ref[0, s], 16), group), slice(None)

    def scores_of(s):
        q = jnp.concatenate([qs_ref[rows_of(s, h)] for h in range(heads)], axis=0)
        return lax.dot_general(q, slots_of(s, 0), NT, preferred_element_type=F32)

    def weigh(s, scores, shifted):
        seen = [jnp.where(m, 1.0, 0.0).astype(BF16) for m in masks(s)]
        weights = []
        for h in range(heads):
            row = []
            for n in range(PLANE):
                part = scores[h * group : (h + 1) * group, n * LANES : (n + 1) * LANES]
                if shifted:
                    part = jnp.minimum(part - top_ref[rows_of(s, h)], 0.0)
                row.append(jnp.exp2(part).astype(BF16) * seen[n])
            weights.append(jnp.concatenate(row, axis=1))
        out = jnp.dot(
            jnp.concatenate(weights, axis=0),
            jnp.concatenate([slots_of(s, slots), ones], axis=1),
            preferred_element_type=F32,
        )
        for h in range(heads):
            acc_ref[rows_of(s, h)] += out[h * group : (h + 1) * group, :HD]
            total_ref[rows_of(s, h)] += out[h * group : (h + 1) * group, HD:]

    wide = iota((padded, LANES), 1)

    @pl.when(large)
    def _():
        top_ref[...] = jnp.full(top_ref.shape, NEG, F32)

        def look(s, carry):
            scores = scores_of(s)
            seen = masks(s)
            for h in range(heads):
                best = top_ref[rows_of(s, h)]
                for n in range(PLANE):
                    part = scores[h * group : (h + 1) * group, n * LANES : (n + 1) * LANES]
                    best = jnp.maximum(best, jnp.where(seen[n], part, NEG))
                top_ref[rows_of(s, h)] = best
            return carry

        lax.fori_loop(0, made, look, 0)
        block = jnp.zeros((padded, LANES), F32)
        for h in range(heads):
            best = jnp.max(top_ref[h], axis=1, keepdims=True)
            best = jnp.broadcast_to(jnp.where(best < 0.5 * NEG, 0.0, best), top_ref.shape[1:])
            top_ref[h] = best
            block = jnp.where(wide == h, best[:padded], block)
        shift_ref[...] = block

        def step(s, carry):
            weigh(s, scores_of(s), True)
            return carry

        lax.fori_loop(0, made, step, 0)

    @pl.when(jnp.logical_not(large))
    def _():
        shift_ref[...] = jnp.zeros(shift_ref.shape, F32)
        score_a[...] = scores_of(0)

        def pair(i, carry):
            score_b[...] = scores_of(2 * i + 1)
            weigh(2 * i, score_a, False)
            score_a[...] = scores_of(2 * i + 2)
            weigh(2 * i + 1, score_b, False)
            return carry

        lax.fori_loop(0, (made + 1) // 2, pair, 0)

    totals = jnp.zeros((padded, LANES), F32)
    for h in range(heads):
        total = total_ref[h, 0:padded, :]
        totals = jnp.where(wide == h, total, totals)
        scale = 1.0 / jnp.where(total > 0.0, total, 1.0)
        os_ref[:, h * HD : (h + 1) * HD] = (acc_ref[h, 0:padded, :] * scale).astype(BF16)
    some = totals > 0.0
    shares = jnp.where(some, shift_ref[...] + jnp.log2(jnp.where(some, totals, 1.0)), NEG)
    os_ref[:, width:] = three_parts(shares, wide, heads).astype(BF16)
    out = jnp.dot(back_ref[...], os_ref[...], preferred_element_type=F32).astype(BF16)
    for n in range(len(o_refs)):
        o_refs[n][...] = out[n * each : (n + 1) * each, :]


def three_parts(block, wide, heads):
    high = block.astype(BF16).astype(F32)
    middle = (block - high).astype(BF16).astype(F32)
    low = block - high - middle
    out = jnp.where(wide < heads, high, 0.0)
    out = jnp.where((wide >= heads) & (wide < 2 * heads), pltpu.roll(middle, heads, 1), out)
    return jnp.where(
        (wide >= 2 * heads) & (wide < 3 * heads), pltpu.roll(low, 2 * heads, 1), out
    )


def shares_of(ref, heads, rows=slice(None)):
    lab = ref[rows, heads * HD :].astype(F32)
    return lab + pltpu.roll(lab, LANES - heads, 1) + pltpu.roll(lab, LANES - 2 * heads, 1)


def joined(terms, heads):
    shares = [shares_of(ref, heads, rows) for ref, rows in terms]
    best = functools.reduce(jnp.maximum, shares)
    weights = [jnp.exp2(s - best) for s in shares]
    total = sum(weights)
    scale = 1.0 / total
    weights = [w * scale for w in weights]
    outs = []
    for h in range(heads):
        at = slice(h * HD, (h + 1) * HD)
        acc = None
        for w, (ref, rows) in zip(weights, terms):
            term = w[:, h : h + 1] * ref[rows, at].astype(F32)
            acc = term if acc is None else acc + term
        outs.append(acc.astype(BF16))
    return outs, best + jnp.log2(total)


def merge_kernel(up1, down1, up2, down2, from_down, from_up, o_up1, o_down1, o_up2, o_down2):
    tokens = up1.shape[0]
    half = tokens // 2
    heads = (up1.shape[1] - LANES) // HD
    first, second, both = slice(0, half), slice(half, tokens), slice(0, tokens)
    tail = slice(tokens, tokens + half)

    def put(ref, rows, terms):
        outs, share = joined(terms, heads)
        for h in range(heads):
            ref[rows, h * HD : (h + 1) * HD] = outs[h]
        ref[rows, heads * HD :] = three_parts(share, iota(share.shape, 1), heads).astype(BF16)

    put(o_up2, first, [(up2, first), (from_down, tail)])
    o_up2[second, :] = up2[second, :]
    put(o_down2, second, [(down2, second), (from_up, tail)])
    o_down2[first, :] = down2[first, :]
    put(o_up1, both, [(up1, both), (from_down, both)])
    put(o_down1, both, [(down1, both), (from_up, both)])


def combine_kernel(*refs):
    parts, o_ref = refs[:-1], refs[-1]
    heads = o_ref.shape[1] // HD
    outs, _ = joined([(ref, slice(None)) for ref in parts], heads)
    for h in range(heads):
        o_ref[:, h * HD : (h + 1) * HD] = outs[h]


def params(size=VMEM_BYTES):
    return pltpu.CompilerParams(vmem_limit_bytes=size)


def cost(microseconds):
    return pl.CostEstimate(
        flops=int(microseconds * 1.0e9), bytes_accessed=int(microseconds * 3.0e6), transcendentals=0
    )


def on_device(queries, keys, values, key_segment, key_position, query_segment, query_position):
    cycle = lax.axis_size("ctx")
    planes = cycle // PLANE
    tokens, width = queries.shape
    slots = keys.shape[0]
    wide = width + LANES
    kv, qp = pl.pallas_call(
        pack_kernel,
        out_shape=(
            jax.ShapeDtypeStruct((2 * slots + 32, HD), BF16),
            jax.ShapeDtypeStruct((tokens, wide), BF16),
        ),
        in_specs=[pl.BlockSpec(memory_space=pltpu.HBM)] * 7,
        scratch_shapes=[
            pltpu.VMEM((tokens, width), BF16),
            pltpu.VMEM((slots, HD), BF16),
            pltpu.VMEM((slots, HD), BF16),
            pltpu.VMEM((slots // LANES, LANES), jnp.int32),
            pltpu.VMEM((slots // LANES, LANES), jnp.int32),
            pltpu.VMEM((1, tokens), jnp.int32),
            pltpu.VMEM((1, tokens), jnp.int32),
            pltpu.SemaphoreType.DMA((7,)),
        ],
        cost_estimate=cost(3),
        compiler_params=params(ALL_VMEM),
        name="pack",
    )(
        queries, keys, values,
        key_segment.reshape(slots // LANES, LANES), key_position.reshape(slots // LANES, LANES),
        query_segment.reshape(1, tokens), query_position.reshape(1, tokens),
    )

    def swapped(x, bits):
        return lax.ppermute(x, "ctx", [(i, i ^ bits) for i in range(cycle)])

    kv_y = swapped(kv, 2)
    kv_c = swapped(kv, 1)

    def moved(x, steps):
        return lax.ppermute(x, "ctx", [(i, (i + PLANE * steps) % cycle) for i in range(cycle)])

    half = tokens // 2
    up = [qp, moved(qp, 1)]
    down = [qp, moved(qp, -1)]
    up.append(moved(up[1], 1))
    down.append(moved(down[1], -1))
    kv_y, up[2], down[2] = lax.optimization_barrier((kv_y, up[2], down[2]))
    up.append(moved(up[2], 1))
    down.append(moved(down[2], -1))
    kv_yc = swapped(kv_y, 1)

    chunks = (PLANE * slots + PLANE * REQS * 15) // LANES + PLANE * REQS
    smem = pl.BlockSpec(memory_space=pltpu.SMEM)
    vmem = pl.BlockSpec(memory_space=pltpu.VMEM)
    blocks = (kv, kv_c, kv_y, kv_yc)
    kk, whence, meta, norm = pl.pallas_call(
        table_kernel,
        out_shape=(
            jax.ShapeDtypeStruct((chunks * PLANE, LANES), F32),
            jax.ShapeDtypeStruct((PLANE, chunks), jnp.int32),
            jax.ShapeDtypeStruct((2, REQS), jnp.int32),
            jax.ShapeDtypeStruct((8, LANES), F32),
        ),
        out_specs=(vmem, smem, smem, vmem),
        scratch_shapes=[
            pltpu.VMEM((PLANE * 8, slots // LANES, LANES), F32),
            pltpu.VMEM((16, LANES), jnp.int32),
            pltpu.SMEM((16, LANES), jnp.int32),
            pltpu.SemaphoreType.DMA,
        ],
        cost_estimate=cost(2),
        compiler_params=params(),
        name="table",
    )(*blocks)

    heads = width // HD
    up_half, down_half = up[-1][:half], down[-1][half:]
    far = jnp.concatenate([moved(up_half, 1), moved(down_half, -1)], axis=0)

    def order(blocks, group, name):
        everyone = len(blocks) * tokens
        padded = everyone + REQS * 16
        return pl.pallas_call(
            functools.partial(order_kernel, group),
            out_shape=(
                jax.ShapeDtypeStruct((heads, padded + group, HD), BF16),
                jax.ShapeDtypeStruct((padded + group, LANES), F32),
                jax.ShapeDtypeStruct((everyone, padded), BF16),
                jax.ShapeDtypeStruct((2, REQS), jnp.int32),
                jax.ShapeDtypeStruct((8, LANES), F32),
            ),
            out_specs=(vmem, vmem, vmem, smem, vmem),
            scratch_shapes=[pltpu.VMEM((everyone, wide), BF16)],
            cost_estimate=cost(2),
            compiler_params=params(),
            name=name,
        )(*blocks)

    def attend(count, ordered, group, after, name):
        everyone = count * tokens
        padded = everyone + REQS * 16
        held = (heads, padded + group, LANES)
        most = (everyone // group + REQS) * chunks + 3
        return pl.pallas_call(
            functools.partial(attend_kernel, group),
            out_shape=[jax.ShapeDtypeStruct((tokens, wide), BF16)] * count,
            in_specs=[vmem, vmem, vmem, smem, vmem, vmem, vmem, vmem, vmem]
            + [vmem, smem, smem, vmem, pl.BlockSpec(memory_space=pl.ANY)],
            scratch_shapes=[
                pltpu.VMEM((padded, wide), BF16),
                pltpu.VMEM(held, F32),
                pltpu.VMEM(held, F32),
                pltpu.VMEM(held, F32),
                pltpu.VMEM((padded, LANES), F32),
                pltpu.VMEM((heads * group, CHUNK), F32),
                pltpu.VMEM((heads * group, CHUNK), F32),
                pltpu.SMEM((3, most), jnp.int32),
            ],
            cost_estimate=cost(2 * count),
            compiler_params=params(),
            name=name,
        )(*ordered, *blocks, kk, whence, meta, norm, after)

    near = order([qp, up[1], down[1], up[2], down[2]], NEAR_GROUP, "order_near")
    distant = order([up[3], down[3], far], FAR_GROUP, "order_far")
    from3, to3, across = attend(3, distant, FAR_GROUP, norm, "attend_far")
    send_down = jnp.concatenate([from3, across[half:]], axis=0)
    send_up = jnp.concatenate([to3, across[:half]], axis=0)
    from_up = moved(send_down, -2)
    from_down = moved(send_up, 2)
    own, below1, above1, below2, above2 = attend(5, near, NEAR_GROUP, across, "attend_near")
    up1, down1, up2, down2 = pl.pallas_call(
        merge_kernel,
        out_shape=[jax.ShapeDtypeStruct((tokens, wide), BF16)] * 4,
        cost_estimate=cost(2),
        compiler_params=params(),
        name="merge",
    )(above1, below1, above2, below2, from_down, from_up)
    got = [own, moved(up2, 2), moved(down2, -2), moved(up1, 1), moved(down1, -1)]
    return pl.pallas_call(
        combine_kernel,
        out_shape=jax.ShapeDtypeStruct((tokens, width), BF16),
        compiler_params=params(),
        name="combine",
    )(*got)


def solution(mesh):
    placed = (
        P("ctx", "tp"),
        P("ctx", "tp"),
        P("ctx", "tp"),
        P("ctx"),
        P("ctx"),
        P("ctx"),
        P("ctx"),
    )
    return jax.shard_map(
        on_device, mesh=mesh, in_specs=placed, out_specs=P("ctx", "tp"), check_vma=False
    )
```

```python
import functools
import math

import jax
import jax.numpy as jnp
from jax import lax
from jax.experimental import pallas as pl
from jax.experimental.pallas import tpu as pltpu
from jax.sharding import PartitionSpec as P

HD = 128
LANES = 128
REQS = 8
SPAN = 16384
BIG = 1e9
NEG = -1e30
SCALE2 = math.log2(math.e) / math.sqrt(HD)
LN2 = math.log(2.0)
PLANE = 4
CHUNK = PLANE * LANES
NEAR_GROUP = 48
FAR_GROUP = 32
VMEM_BYTES = 32 * 1024 * 1024
ALL_VMEM = 62 * 1024 * 1024
F32 = jnp.float32
BF16 = jnp.bfloat16

NT = (((1,), (1,)), ((), ()))


def iota(shape, dim):
    return lax.broadcasted_iota(jnp.int32, shape, dim)


def pack_kernel(*refs):
    far, (kv_ref, qp_ref), near, sems = refs[:7], refs[7:9], refs[9:16], refs[16]
    copies = [pltpu.make_async_copy(a, b, sems.at[n]) for n, (a, b) in enumerate(zip(far, near))]
    for copy in copies:
        copy.start()
    for copy in copies:
        copy.wait()
    q_ref, k_ref, v_ref, kseg_ref, kpos_ref, qseg_ref, qpos_ref = near
    slots = k_ref.shape[0]
    tiles = slots // LANES
    tokens = q_ref.shape[0]
    width = q_ref.shape[1]

    qseg = qseg_ref[...].astype(F32)
    qhi = (qpos_ref[...] >> 7).astype(F32)
    qlo = (qpos_ref[...] & 127).astype(F32)
    rows = jnp.concatenate([qseg, qhi, qlo, jnp.zeros((LANES - 3, tokens), F32)], axis=0)
    labels = jnp.transpose(rows).astype(BF16)
    qp_ref[:, :width] = q_ref[...]
    qp_ref[:, width:] = labels

    seg = kseg_ref[...]
    pos = kpos_ref[...]
    code = (seg * SPAN + pos).astype(F32)
    ranks = [jnp.zeros((1, LANES), F32) for _ in range(tiles)]
    for t in range(tiles):
        col = jnp.transpose(jnp.broadcast_to(code[t : t + 1, :], (LANES, LANES)))
        for u in range(tiles):
            less = jnp.where(col < code[u : u + 1, :], 1.0, 0.0)
            ranks[u] = ranks[u] + jnp.sum(less, axis=0, keepdims=True)
    rank = jnp.concatenate(ranks, axis=1).astype(jnp.int32)
    place = jnp.where(iota((slots, slots), 0) == rank, 1.0, 0.0).astype(BF16)
    both = jnp.concatenate([k_ref[...], v_ref[...]], axis=1)
    both = jnp.dot(place, both, preferred_element_type=F32).astype(BF16)
    kv_ref[0:slots, :] = both[:, :HD]
    kv_ref[slots : 2 * slots, :] = both[:, HD:]
    flat = lambda x: jnp.concatenate([x[t : t + 1, :] for t in range(tiles)], axis=1)
    labs = jnp.concatenate(
        [flat(seg.astype(F32)), flat((pos >> 7).astype(F32)), flat((pos & 127).astype(F32)),
         jnp.zeros((5, slots), F32)], axis=0)
    moved = lax.dot_general(labs.astype(BF16), place, NT, preferred_element_type=F32)
    parts = [moved[w : w + 1, t * LANES : (t + 1) * LANES] for w in range(3) for t in range(tiles)]
    k = k_ref[...]
    sums = jnp.dot(k * k, jnp.ones((HD, LANES), BF16), preferred_element_type=F32)
    parts.append(jnp.max(sums, axis=0, keepdims=True) * 1.02)
    parts.append(jnp.zeros((31 - 3 * tiles, LANES), F32))
    kv_ref[2 * slots :, :] = jnp.concatenate(parts, axis=0).astype(BF16)


def start_table(blocks, norm_ref, shifted_ref, start_vmem, start_smem, sem):
    slots = (blocks[0].shape[0] - 32) // 2
    tiles = slots // LANES
    lane = iota((tiles, LANES), 1)
    best = jnp.zeros((1, LANES), F32)
    table = jnp.zeros((16, LANES), F32)
    for b in range(PLANE):
        lab = blocks[b][2 * slots : 2 * slots + 32, :].astype(F32)
        code = lab[:tiles] * SPAN + lab[tiles : 2 * tiles] * 128.0 + lab[2 * tiles : 3 * tiles]
        best = jnp.maximum(best, lab[3 * tiles : 3 * tiles + 1])
        below = [
            jnp.sum(jnp.where(code < float(r * SPAN), 1.0, 0.0), axis=0, keepdims=True)
            for r in range(REQS + 1)
        ]
        below.append(jnp.zeros((16 - REQS - 1, LANES), F32))
        counts = jnp.sum(jnp.concatenate(below, axis=0), axis=1, keepdims=True)
        table = jnp.where(iota((16, LANES), 1) == b, counts, table)
    start_vmem[...] = table.astype(jnp.int32)
    copy = pltpu.make_async_copy(start_vmem, start_smem, sem)
    copy.start()
    norm_ref[...] = jnp.broadcast_to(best, norm_ref.shape)
    for b in range(PLANE):
        lab = blocks[b][2 * slots : 2 * slots + 32, :].astype(F32)
        code = lab[:tiles] * SPAN + lab[tiles : 2 * tiles] * 128.0 + lab[2 * tiles : 3 * tiles]
        after = jnp.concatenate([code[1:], code[:1]], axis=0)
        shifted_ref[b * 8] = code
        for n in range(1, 8):
            step = 16 * n
            shifted_ref[b * 8 + n] = jnp.where(
                lane < LANES - step,
                pltpu.roll(code, LANES - step, 1),
                pltpu.roll(after, LANES - step, 1),
            )
    return copy


def finish_table(slots, kk_ref, from_ref, meta_ref, shifted_ref, start_smem):
    lane1 = iota((1, LANES), 1)

    def request(r, made):
        first = (r * SPAN).astype(F32)
        bases = []
        count = jnp.int32(0)
        for b in range(PLANE):
            lo = start_smem[r, b]
            hi = start_smem[r + 1, b]
            base = lo & ~15
            bases.append(base)
            count = jnp.maximum(count, jnp.where(hi > lo, (hi - base + LANES - 1) // LANES, 0))

        def one(j, carry):
            for b in range(PLANE):
                want = bases[b] + j * LANES
                have = jnp.minimum(want, slots - LANES)
                from_ref[b, made + j] = have
                row = shifted_ref[b * 8 + (have % LANES) // 16, pl.ds(have // LANES, 1), :]
                good = (row >= first) & (row < first + SPAN) & (lane1 + have >= want)
                kk_ref[pl.ds((made + j) * PLANE + b, 1), :] = jnp.where(good, row, BIG)
            return carry

        lax.fori_loop(0, count, one, 0)
        meta_ref[0, r] = made
        meta_ref[1, r] = made + count
        return made + count

    lax.fori_loop(0, REQS, request, jnp.int32(0))


def order_kernel(group, *refs):
    order(group, refs[:-6], *refs[-6:])


def order(group, q_refs, qs_ref, qcode_ref, back_ref, span_ref, norm_ref, q_ref):
    each = q_refs[0].shape[0]
    for n, ref in enumerate(q_refs):
        q_ref[n * each : (n + 1) * each, :] = ref[...]
    tokens = q_ref.shape[0]
    heads = qs_ref.shape[0]
    width = heads * HD
    padded = tokens + REQS * 16
    lab = q_ref[:, width:].astype(F32)
    lab_t = jnp.transpose(lab)
    seg_row = lab_t[0:1]
    code_row = seg_row * SPAN + lab_t[1:2] * 128.0 + lab_t[2:3]
    seg_col = lab[:, 0:1]
    code_col = seg_col * SPAN + lab[:, 1:2] * 128.0 + lab[:, 2:3]
    rank_row = jnp.sum(jnp.where(code_col < code_row, 1.0, 0.0), axis=0, keepdims=True)
    rank_col = jnp.sum(jnp.where(code_row < code_col, 1.0, 0.0), axis=1, keepdims=True)
    counts = [
        jnp.sum(jnp.where(seg_row == float(r), 1.0, 0.0), axis=1, keepdims=True) for r in range(REQS)
    ]
    extra = jnp.zeros((1, 1), F32)
    for r in range(REQS):
        rank_row = rank_row + jnp.where(seg_row == float(r), extra, 0.0)
        rank_col = rank_col + jnp.where(seg_col == float(r), extra, 0.0)
        extra = extra + (jnp.ceil(counts[r] * (1.0 / 16.0)) * 16.0 - counts[r])
    used = jnp.int32(0)
    for r in range(REQS):
        count = jnp.max(counts[r]).astype(jnp.int32)
        span_ref[0, r] = used
        span_ref[1, r] = (count + group - 1) // group
        used = used + ((count + 15) // 16) * 16
    place = jnp.where(
        iota((padded, tokens), 0) == rank_row.astype(jnp.int32), 1.0, 0.0
    ).astype(BF16)
    back_ref[...] = jnp.where(
        iota((tokens, padded), 1) == rank_col.astype(jnp.int32), 1.0, 0.0
    ).astype(BF16)
    ones = jnp.ones((HD, LANES), BF16)
    sums = jnp.zeros((padded, LANES), F32)
    for h in range(heads):
        q = jnp.dot(place, q_ref[:, h * HD : (h + 1) * HD], preferred_element_type=F32)
        q = q.astype(BF16)
        qs_ref[h, 0:padded, :] = q
        qs_ref[h, padded:, :] = jnp.zeros((group, HD), BF16)
        sums = jnp.maximum(sums, jnp.dot(q * q, ones, preferred_element_type=F32))
    norm_ref[...] = jnp.broadcast_to(jnp.max(sums, axis=0, keepdims=True), norm_ref.shape)
    lab_s = jnp.dot(place, q_ref[:, width:], preferred_element_type=F32)
    qcode = lab_s[:, 0:1] * SPAN + lab_s[:, 1:2] * 128.0 + lab_s[:, 2:3]
    qcode_ref[0:padded, :] = jnp.broadcast_to(qcode, (padded, LANES))
    qcode_ref[padded:, :] = jnp.zeros((group, LANES), F32)


def near_kernel(group, count, *refs):
    ordered, blocks, table, o_refs = refs[:5], refs[5:9], refs[9:13], refs[14 : 14 + count]
    attend(group, ordered, blocks, table, o_refs, *refs[14 + count :])


def far_kernel(group, count, *refs):
    q_refs, blocks, refs = refs[:count], refs[count : count + PLANE], refs[count + PLANE :]
    o_refs, table, refs = refs[:count], refs[count : count + 4], refs[count + 4 :]
    ordered, q_ref, shifted_ref, start_vmem, start_smem, sem = refs[:5], *refs[5:10]
    kk_ref, from_ref, meta_ref, norm_ref = table
    slots = (blocks[0].shape[0] - 32) // 2
    copy = start_table(blocks, norm_ref, shifted_ref, start_vmem, start_smem, sem)
    order(group, q_refs, *ordered, q_ref)
    copy.wait()
    finish_table(slots, kk_ref, from_ref, meta_ref, shifted_ref, start_smem)
    attend(group, ordered, blocks, table, o_refs, *refs[10:])


def attend(
    group, ordered, blocks, table, o_refs,
    os_ref, acc_ref, total_ref, top_ref, shift_ref, score_a, score_b, steps_ref,
):
    qs_ref, qcode_ref, back_ref, span_ref, qnorm_ref = ordered
    kk_ref, from_ref, meta_ref, norm_ref = table
    heads = qs_ref.shape[0]
    width = heads * HD
    tokens, padded = back_ref.shape
    each = o_refs[0].shape[0]

    made = jnp.int32(0)
    for r in range(REQS):
        chunk_lo = meta_ref[0, r]
        chunk_hi = meta_ref[1, r]

        def one_group(g, made, r=r, chunk_lo=chunk_lo, chunk_hi=chunk_hi):
            def one_chunk(c, made):
                steps_ref[0, made] = span_ref[0, r] + g * group
                steps_ref[1, made] = c
                steps_ref[2, made] = r * SPAN
                return made + 1

            return lax.fori_loop(chunk_lo, chunk_hi, one_chunk, made)

        made = lax.fori_loop(0, span_ref[1, r], one_group, made)
    for n in range(3):
        steps_ref[0, made + n] = 0
        steps_ref[1, made + n] = 0
        steps_ref[2, made + n] = REQS * SPAN
    acc_ref[...] = jnp.zeros(acc_ref.shape, F32)
    total_ref[...] = jnp.zeros(total_ref.shape, F32)

    large = jnp.max(qnorm_ref[...] * norm_ref[...]) * (1.05 * SCALE2 * SCALE2) > 80.0 * 80.0

    slots = (blocks[0].shape[0] - 32) // 2
    ones = jnp.ones((CHUNK, LANES), BF16)

    def masks(s):
        row0 = pl.multiple_of(steps_ref[0, s], 16)
        first = steps_ref[2, s].astype(F32)
        code = qcode_ref[pl.ds(row0, group), :]
        limit = jnp.where((code >= first) & (code < first + SPAN), code, -1.0)
        row = steps_ref[1, s] * PLANE
        return [kk_ref[pl.ds(row + b, 1), :] <= limit for b in range(PLANE)]

    def slots_of(s, base):
        c = steps_ref[1, s]
        return jnp.concatenate(
            [
                blocks[b][pl.ds(pl.multiple_of(base + from_ref[b, c], 16), LANES), :]
                for b in range(PLANE)
            ],
            axis=0,
        )

    def rows_of(s, h):
        return h, pl.ds(pl.multiple_of(steps_ref[0, s], 16), group), slice(None)

    def scores_of(s):
        q = jnp.concatenate([qs_ref[rows_of(s, h)] for h in range(heads)], axis=0)
        return lax.dot_general(q, slots_of(s, 0), NT, preferred_element_type=F32) * SCALE2

    def weigh(s, scores, shifted):
        seen = [jnp.where(m, 1.0, 0.0).astype(BF16) for m in masks(s)]
        weights = []
        for h in range(heads):
            row = []
            for n in range(PLANE):
                part = scores[h * group : (h + 1) * group, n * LANES : (n + 1) * LANES]
                if shifted:
                    part = jnp.minimum(part - top_ref[rows_of(s, h)], 0.0)
                row.append(jnp.exp2(part).astype(BF16) * seen[n])
            weights.append(jnp.concatenate(row, axis=1))
        out = jnp.dot(
            jnp.concatenate(weights, axis=0),
            jnp.concatenate([slots_of(s, slots), ones], axis=1),
            preferred_element_type=F32,
        )
        for h in range(heads):
            acc_ref[rows_of(s, h)] += out[h * group : (h + 1) * group, :HD]
            total_ref[rows_of(s, h)] += out[h * group : (h + 1) * group, HD:]

    wide = iota((padded, LANES), 1)

    @pl.when(large)
    def _():
        top_ref[...] = jnp.full(top_ref.shape, NEG, F32)

        def look(s, carry):
            scores = scores_of(s)
            seen = masks(s)
            for h in range(heads):
                best = top_ref[rows_of(s, h)]
                for n in range(PLANE):
                    part = scores[h * group : (h + 1) * group, n * LANES : (n + 1) * LANES]
                    best = jnp.maximum(best, jnp.where(seen[n], part, NEG))
                top_ref[rows_of(s, h)] = best
            return carry

        lax.fori_loop(0, made, look, 0)
        block = jnp.zeros((padded, LANES), F32)
        for h in range(heads):
            best = jnp.max(top_ref[h], axis=1, keepdims=True)
            best = jnp.broadcast_to(jnp.where(best < 0.5 * NEG, 0.0, best), top_ref.shape[1:])
            top_ref[h] = best
            block = jnp.where(wide == h, best[:padded], block)
        shift_ref[...] = block

        def step(s, carry):
            weigh(s, scores_of(s), True)
            return carry

        lax.fori_loop(0, made, step, 0)

    @pl.when(jnp.logical_not(large))
    def _():
        shift_ref[...] = jnp.zeros(shift_ref.shape, F32)
        score_a[...] = scores_of(0)

        def pair(i, carry):
            score_b[...] = scores_of(2 * i + 1)
            weigh(2 * i, score_a, False)
            score_a[...] = scores_of(2 * i + 2)
            weigh(2 * i + 1, score_b, False)
            return carry

        lax.fori_loop(0, (made + 1) // 2, pair, 0)

    totals = jnp.zeros((padded, LANES), F32)
    for h in range(heads):
        total = total_ref[h, 0:padded, :]
        totals = jnp.where(wide == h, total, totals)
        scale = 1.0 / jnp.where(total > 0.0, total, 1.0)
        os_ref[:, h * HD : (h + 1) * HD] = (acc_ref[h, 0:padded, :] * scale).astype(BF16)
    some = totals > 0.0
    shares = jnp.where(some, shift_ref[...] + jnp.log2(jnp.where(some, totals, 1.0)), NEG)
    os_ref[:, width:] = three_parts(shares, wide, heads).astype(BF16)
    out = jnp.dot(back_ref[...], os_ref[...], preferred_element_type=F32).astype(BF16)
    for n in range(len(o_refs)):
        o_refs[n][...] = out[n * each : (n + 1) * each, :]


def three_parts(block, wide, heads):
    high = block.astype(BF16).astype(F32)
    middle = (block - high).astype(BF16).astype(F32)
    low = block - high - middle
    out = jnp.where(wide < heads, high, 0.0)
    out = jnp.where((wide >= heads) & (wide < 2 * heads), pltpu.roll(middle, heads, 1), out)
    return jnp.where(
        (wide >= 2 * heads) & (wide < 3 * heads), pltpu.roll(low, 2 * heads, 1), out
    )


def shares_of(ref, heads, rows=slice(None)):
    lab = ref[rows, heads * HD :].astype(F32)
    return lab + pltpu.roll(lab, LANES - heads, 1) + pltpu.roll(lab, LANES - 2 * heads, 1)


def joined(terms, heads):
    shares = [shares_of(ref, heads, rows) for ref, rows in terms]
    best = functools.reduce(jnp.maximum, shares)
    weights = [jnp.exp2(s - best) for s in shares]
    total = sum(weights)
    scale = 1.0 / total
    weights = [w * scale for w in weights]
    outs = []
    for h in range(heads):
        at = slice(h * HD, (h + 1) * HD)
        acc = None
        for w, (ref, rows) in zip(weights, terms):
            term = w[:, h : h + 1] * ref[rows, at].astype(F32)
            acc = term if acc is None else acc + term
        outs.append(acc.astype(BF16))
    return outs, best + jnp.log2(total)


def merge_kernel(up1, down1, up2, down2, from_down, from_up, o_up1, o_down1, o_up2, o_down2):
    tokens = up1.shape[0]
    half = tokens // 2
    heads = (up1.shape[1] - LANES) // HD
    first, second, both = slice(0, half), slice(half, tokens), slice(0, tokens)
    tail = slice(tokens, tokens + half)

    def put(ref, rows, terms):
        outs, share = joined(terms, heads)
        for h in range(heads):
            ref[rows, h * HD : (h + 1) * HD] = outs[h]
        ref[rows, heads * HD :] = three_parts(share, iota(share.shape, 1), heads).astype(BF16)

    put(o_up2, first, [(up2, first), (from_down, tail)])
    o_up2[second, :] = up2[second, :]
    put(o_down2, second, [(down2, second), (from_up, tail)])
    o_down2[first, :] = down2[first, :]
    put(o_up1, both, [(up1, both), (from_down, both)])
    put(o_down1, both, [(down1, both), (from_up, both)])


def combine_kernel(*refs):
    parts, o_ref = refs[:-1], refs[-1]
    heads = o_ref.shape[1] // HD
    outs, _ = joined([(ref, slice(None)) for ref in parts], heads)
    for h in range(heads):
        o_ref[:, h * HD : (h + 1) * HD] = outs[h]


def params(size=VMEM_BYTES):
    return pltpu.CompilerParams(vmem_limit_bytes=size)


def cost(microseconds):
    return pl.CostEstimate(
        flops=int(microseconds * 1.0e9), bytes_accessed=int(microseconds * 3.0e6), transcendentals=0
    )


def on_device(queries, keys, values, key_segment, key_position, query_segment, query_position):
    cycle = lax.axis_size("ctx")
    planes = cycle // PLANE
    tokens, width = queries.shape
    slots = keys.shape[0]
    wide = width + LANES
    kv, qp = pl.pallas_call(
        pack_kernel,
        out_shape=(
            jax.ShapeDtypeStruct((2 * slots + 32, HD), BF16),
            jax.ShapeDtypeStruct((tokens, wide), BF16),
        ),
        in_specs=[pl.BlockSpec(memory_space=pltpu.HBM)] * 7,
        scratch_shapes=[
            pltpu.VMEM((tokens, width), BF16),
            pltpu.VMEM((slots, HD), BF16),
            pltpu.VMEM((slots, HD), BF16),
            pltpu.VMEM((slots // LANES, LANES), jnp.int32),
            pltpu.VMEM((slots // LANES, LANES), jnp.int32),
            pltpu.VMEM((1, tokens), jnp.int32),
            pltpu.VMEM((1, tokens), jnp.int32),
            pltpu.SemaphoreType.DMA((7,)),
        ],
        cost_estimate=cost(3),
        compiler_params=params(ALL_VMEM),
        name="pack",
    )(
        queries, keys, values,
        key_segment.reshape(slots // LANES, LANES), key_position.reshape(slots // LANES, LANES),
        query_segment.reshape(1, tokens), query_position.reshape(1, tokens),
    )

    def swapped(x, bits):
        return lax.ppermute(x, "ctx", [(i, i ^ bits) for i in range(cycle)])

    kv_y = swapped(kv, 2)
    kv_c = swapped(kv, 1)

    def moved(x, steps):
        return lax.ppermute(x, "ctx", [(i, (i + PLANE * steps) % cycle) for i in range(cycle)])

    half = tokens // 2
    up = [qp, moved(qp, 1)]
    down = [qp, moved(qp, -1)]
    up.append(moved(up[1], 1))
    down.append(moved(down[1], -1))
    kv_y, up[2], down[2] = lax.optimization_barrier((kv_y, up[2], down[2]))
    up.append(moved(up[2], 1))
    down.append(moved(down[2], -1))
    kv_yc = swapped(kv_y, 1)
    far = jnp.concatenate([moved(up[3][:half], 1), moved(down[3][half:], -1)], axis=0)

    chunks = (PLANE * slots + PLANE * REQS * 15) // LANES + PLANE * REQS
    smem = pl.BlockSpec(memory_space=pltpu.SMEM)
    vmem = pl.BlockSpec(memory_space=pltpu.VMEM)
    anywhere = pl.BlockSpec(memory_space=pl.ANY)
    blocks = (kv, kv_c, kv_y, kv_yc)
    heads = width // HD
    table_like = (
        jax.ShapeDtypeStruct((chunks * PLANE, LANES), F32),
        jax.ShapeDtypeStruct((PLANE, chunks), jnp.int32),
        jax.ShapeDtypeStruct((2, REQS), jnp.int32),
        jax.ShapeDtypeStruct((8, LANES), F32),
    )
    table_specs = (vmem, smem, smem, vmem)
    ordered_specs = (vmem, vmem, vmem, smem, vmem)
    result = jax.ShapeDtypeStruct((tokens, wide), BF16)

    def ordered_like(count, group):
        padded = count * tokens + REQS * 16
        return (
            jax.ShapeDtypeStruct((heads, padded + group, HD), BF16),
            jax.ShapeDtypeStruct((padded + group, LANES), F32),
            jax.ShapeDtypeStruct((count * tokens, padded), BF16),
            jax.ShapeDtypeStruct((2, REQS), jnp.int32),
            jax.ShapeDtypeStruct((8, LANES), F32),
        )

    def attend_scratch(count, group):
        padded = count * tokens + REQS * 16
        held = (heads, padded + group, LANES)
        most = (count * tokens // group + REQS) * chunks + 3
        return [
            pltpu.VMEM((padded, wide), BF16),
            pltpu.VMEM(held, F32),
            pltpu.VMEM(held, F32),
            pltpu.VMEM(held, F32),
            pltpu.VMEM((padded, LANES), F32),
            pltpu.VMEM((heads * group, CHUNK), F32),
            pltpu.VMEM((heads * group, CHUNK), F32),
            pltpu.SMEM((3, most), jnp.int32),
        ]

    near_blocks = [qp, up[1], down[1], up[2], down[2]]
    far_blocks = [up[3], down[3], far]
    ordered = pl.pallas_call(
        functools.partial(order_kernel, NEAR_GROUP),
        out_shape=ordered_like(5, NEAR_GROUP),
        out_specs=ordered_specs,
        scratch_shapes=[pltpu.VMEM((5 * tokens, wide), BF16)],
        cost_estimate=cost(2),
        compiler_params=params(),
        name="order_near",
    )(*near_blocks)
    in_vmem = [pltpu.VMEM(like.shape, like.dtype) for like in ordered_like(3, FAR_GROUP)]
    in_vmem[3] = pltpu.SMEM((2, REQS), jnp.int32)
    from3, to3, across, *table = pl.pallas_call(
        functools.partial(far_kernel, FAR_GROUP, 3),
        out_shape=(result,) * 3 + table_like,
        in_specs=[vmem] * 7,
        out_specs=(vmem,) * 3 + table_specs,
        scratch_shapes=in_vmem
        + [
            pltpu.VMEM((3 * tokens, wide), BF16),
            pltpu.VMEM((PLANE * 8, slots // LANES, LANES), F32),
            pltpu.VMEM((16, LANES), jnp.int32),
            pltpu.SMEM((16, LANES), jnp.int32),
            pltpu.SemaphoreType.DMA,
        ]
        + attend_scratch(3, FAR_GROUP),
        cost_estimate=cost(8),
        compiler_params=params(),
        name="attend_far",
    )(*far_blocks, *blocks)

    send_down = jnp.concatenate([from3, across[half:]], axis=0)
    send_up = jnp.concatenate([to3, across[:half]], axis=0)
    from_up = moved(send_down, -2)
    from_down = moved(send_up, 2)
    own, below1, above1, below2, above2 = pl.pallas_call(
        functools.partial(near_kernel, NEAR_GROUP, 5),
        out_shape=(result,) * 5,
        in_specs=[*ordered_specs] + [vmem] * PLANE + [*table_specs, anywhere],
        scratch_shapes=attend_scratch(5, NEAR_GROUP),
        cost_estimate=cost(8),
        compiler_params=params(),
        name="attend_near",
    )(*ordered, *blocks, *table, across)
    up1, down1, up2, down2 = pl.pallas_call(
        merge_kernel,
        out_shape=[jax.ShapeDtypeStruct((tokens, wide), BF16)] * 4,
        cost_estimate=cost(2),
        compiler_params=params(),
        name="merge",
    )(above1, below1, above2, below2, from_down, from_up)
    got = [own, moved(up2, 2), moved(down2, -2), moved(up1, 1), moved(down1, -1)]
    return pl.pallas_call(
        combine_kernel,
        out_shape=jax.ShapeDtypeStruct((tokens, width), BF16),
        compiler_params=params(),
        name="combine",
    )(*got)


def solution(mesh):
    placed = (
        P("ctx", "tp"),
        P("ctx", "tp"),
        P("ctx", "tp"),
        P("ctx"),
        P("ctx"),
        P("ctx"),
        P("ctx"),
    )
    return jax.shard_map(
        on_device, mesh=mesh, in_specs=placed, out_specs=P("ctx", "tp"), check_vma=False
    )
```

```python
import functools
import math

import jax
import jax.numpy as jnp
from jax import lax
from jax.experimental import pallas as pl
from jax.experimental.pallas import tpu as pltpu
from jax.sharding import PartitionSpec as P

HD = 128
LANES = 128
REQS = 8
SPAN = 16384
BIG = 1e9
NEG = -1e30
SCALE2 = math.log2(math.e) / math.sqrt(HD)
LN2 = math.log(2.0)
PLANE = 4
CHUNK = PLANE * LANES
NEAR_GROUP = 48
FAR_GROUP = 32
VMEM_BYTES = 32 * 1024 * 1024
ALL_VMEM = 62 * 1024 * 1024
F32 = jnp.float32
BF16 = jnp.bfloat16

NT = (((1,), (1,)), ((), ()))


def iota(shape, dim):
    return lax.broadcasted_iota(jnp.int32, shape, dim)


def pack_kernel(*refs):
    far, (kv_ref, qp_ref), near, sems = refs[:7], refs[7:9], refs[9:16], refs[16]
    copies = [pltpu.make_async_copy(a, b, sems.at[n]) for n, (a, b) in enumerate(zip(far, near))]
    for copy in copies:
        copy.start()
    for copy in copies:
        copy.wait()
    q_ref, k_ref, v_ref, kseg_ref, kpos_ref, qseg_ref, qpos_ref = near
    slots = k_ref.shape[0]
    tiles = slots // LANES
    tokens = q_ref.shape[0]
    width = q_ref.shape[1]

    qseg = qseg_ref[...].astype(F32)
    qhi = (qpos_ref[...] >> 7).astype(F32)
    qlo = (qpos_ref[...] & 127).astype(F32)
    rows = jnp.concatenate([qseg, qhi, qlo, jnp.zeros((LANES - 3, tokens), F32)], axis=0)
    labels = jnp.transpose(rows).astype(BF16)
    qp_ref[:, :width] = q_ref[...]
    qp_ref[:, width:] = labels

    seg = kseg_ref[...]
    pos = kpos_ref[...]
    code = (seg * SPAN + pos).astype(F32)
    ranks = [jnp.zeros((1, LANES), F32) for _ in range(tiles)]
    for t in range(tiles):
        col = jnp.transpose(jnp.broadcast_to(code[t : t + 1, :], (LANES, LANES)))
        for u in range(tiles):
            less = jnp.where(col < code[u : u + 1, :], 1.0, 0.0)
            ranks[u] = ranks[u] + jnp.sum(less, axis=0, keepdims=True)
    rank = jnp.concatenate(ranks, axis=1).astype(jnp.int32)
    place = jnp.where(iota((slots, slots), 0) == rank, 1.0, 0.0).astype(BF16)
    both = jnp.concatenate([k_ref[...], v_ref[...]], axis=1)
    both = jnp.dot(place, both, preferred_element_type=F32).astype(BF16)
    kv_ref[0:slots, :] = both[:, :HD]
    kv_ref[slots : 2 * slots, :] = both[:, HD:]
    flat = lambda x: jnp.concatenate([x[t : t + 1, :] for t in range(tiles)], axis=1)
    labs = jnp.concatenate(
        [flat(seg.astype(F32)), flat((pos >> 7).astype(F32)), flat((pos & 127).astype(F32)),
         jnp.zeros((5, slots), F32)], axis=0)
    moved = lax.dot_general(labs.astype(BF16), place, NT, preferred_element_type=F32)
    parts = [moved[w : w + 1, t * LANES : (t + 1) * LANES] for w in range(3) for t in range(tiles)]
    k = k_ref[...]
    sums = jnp.dot(k * k, jnp.ones((HD, LANES), BF16), preferred_element_type=F32)
    parts.append(jnp.max(sums, axis=0, keepdims=True) * 1.02)
    parts.append(jnp.zeros((31 - 3 * tiles, LANES), F32))
    kv_ref[2 * slots :, :] = jnp.concatenate(parts, axis=0).astype(BF16)


def start_table(blocks, norm_ref, shifted_ref, start_vmem, start_smem, sem):
    slots = (blocks[0].shape[0] - 32) // 2
    tiles = slots // LANES
    lane = iota((tiles, LANES), 1)
    best = jnp.zeros((1, LANES), F32)
    table = jnp.zeros((16, LANES), F32)
    for b in range(PLANE):
        lab = blocks[b][2 * slots : 2 * slots + 32, :].astype(F32)
        code = lab[:tiles] * SPAN + lab[tiles : 2 * tiles] * 128.0 + lab[2 * tiles : 3 * tiles]
        best = jnp.maximum(best, lab[3 * tiles : 3 * tiles + 1])
        below = [
            jnp.sum(jnp.where(code < float(r * SPAN), 1.0, 0.0), axis=0, keepdims=True)
            for r in range(REQS + 1)
        ]
        below.append(jnp.zeros((16 - REQS - 1, LANES), F32))
        counts = jnp.sum(jnp.concatenate(below, axis=0), axis=1, keepdims=True)
        table = jnp.where(iota((16, LANES), 1) == b, counts, table)
    start_vmem[...] = table.astype(jnp.int32)
    copy = pltpu.make_async_copy(start_vmem, start_smem, sem)
    copy.start()
    norm_ref[...] = jnp.broadcast_to(best, norm_ref.shape)
    for b in range(PLANE):
        lab = blocks[b][2 * slots : 2 * slots + 32, :].astype(F32)
        code = lab[:tiles] * SPAN + lab[tiles : 2 * tiles] * 128.0 + lab[2 * tiles : 3 * tiles]
        after = jnp.concatenate([code[1:], code[:1]], axis=0)
        shifted_ref[b * 8] = code
        for n in range(1, 8):
            step = 16 * n
            shifted_ref[b * 8 + n] = jnp.where(
                lane < LANES - step,
                pltpu.roll(code, LANES - step, 1),
                pltpu.roll(after, LANES - step, 1),
            )
    return copy


def finish_table(slots, kk_ref, from_ref, meta_ref, shifted_ref, start_smem):
    lane1 = iota((1, LANES), 1)

    def request(r, made):
        first = (r * SPAN).astype(F32)
        bases = []
        count = jnp.int32(0)
        for b in range(PLANE):
            lo = start_smem[r, b]
            hi = start_smem[r + 1, b]
            base = lo & ~15
            bases.append(base)
            count = jnp.maximum(count, jnp.where(hi > lo, (hi - base + LANES - 1) // LANES, 0))

        def one(j, carry):
            for b in range(PLANE):
                want = bases[b] + j * LANES
                have = jnp.minimum(want, slots - LANES)
                from_ref[b, made + j] = have
                row = shifted_ref[b * 8 + (have % LANES) // 16, pl.ds(have // LANES, 1), :]
                good = (row >= first) & (row < first + SPAN) & (lane1 + have >= want)
                kk_ref[pl.ds((made + j) * PLANE + b, 1), :] = jnp.where(good, row, BIG)
            return carry

        lax.fori_loop(0, count, one, 0)
        meta_ref[0, r] = made
        meta_ref[1, r] = made + count
        return made + count

    lax.fori_loop(0, REQS, request, jnp.int32(0))


def order_kernel(group, *refs):
    order(group, refs[:-6], *refs[-6:])


def order(group, q_refs, qs_ref, qcode_ref, back_ref, span_ref, norm_ref, q_ref):
    each = q_refs[0].shape[0]
    for n, ref in enumerate(q_refs):
        q_ref[n * each : (n + 1) * each, :] = ref[...]
    tokens = q_ref.shape[0]
    heads = qs_ref.shape[0]
    width = heads * HD
    padded = tokens + REQS * 16
    lab = q_ref[:, width:].astype(F32)
    lab_t = jnp.transpose(lab)
    seg_row = lab_t[0:1]
    code_row = seg_row * SPAN + lab_t[1:2] * 128.0 + lab_t[2:3]
    seg_col = lab[:, 0:1]
    code_col = seg_col * SPAN + lab[:, 1:2] * 128.0 + lab[:, 2:3]
    rank_row = jnp.sum(jnp.where(code_col < code_row, 1.0, 0.0), axis=0, keepdims=True)
    rank_col = jnp.sum(jnp.where(code_row < code_col, 1.0, 0.0), axis=1, keepdims=True)
    counts = [
        jnp.sum(jnp.where(seg_row == float(r), 1.0, 0.0), axis=1, keepdims=True) for r in range(REQS)
    ]
    extra = jnp.zeros((1, 1), F32)
    for r in range(REQS):
        rank_row = rank_row + jnp.where(seg_row == float(r), extra, 0.0)
        rank_col = rank_col + jnp.where(seg_col == float(r), extra, 0.0)
        extra = extra + (jnp.ceil(counts[r] * (1.0 / 16.0)) * 16.0 - counts[r])
    used = jnp.int32(0)
    for r in range(REQS):
        count = jnp.max(counts[r]).astype(jnp.int32)
        span_ref[0, r] = used
        span_ref[1, r] = (count + group - 1) // group
        used = used + ((count + 15) // 16) * 16
    place = jnp.where(
        iota((padded, tokens), 0) == rank_row.astype(jnp.int32), 1.0, 0.0
    ).astype(BF16)
    back_ref[...] = jnp.where(
        iota((tokens, padded), 1) == rank_col.astype(jnp.int32), 1.0, 0.0
    ).astype(BF16)
    ones = jnp.ones((HD, LANES), BF16)
    sums = jnp.zeros((padded, LANES), F32)
    for h in range(heads):
        q = jnp.dot(place, q_ref[:, h * HD : (h + 1) * HD], preferred_element_type=F32)
        q = q.astype(BF16)
        qs_ref[h, 0:padded, :] = q
        qs_ref[h, padded:, :] = jnp.zeros((group, HD), BF16)
        sums = jnp.maximum(sums, jnp.dot(q * q, ones, preferred_element_type=F32))
    norm_ref[...] = jnp.broadcast_to(jnp.max(sums, axis=0, keepdims=True), norm_ref.shape)
    lab_s = jnp.dot(place, q_ref[:, width:], preferred_element_type=F32)
    qcode = lab_s[:, 0:1] * SPAN + lab_s[:, 1:2] * 128.0 + lab_s[:, 2:3]
    qcode_ref[0:padded, :] = jnp.broadcast_to(qcode, (padded, LANES))
    qcode_ref[padded:, :] = jnp.zeros((group, LANES), F32)


def near_kernel(group, count, *refs):
    ordered, blocks, table, o_refs = refs[:5], refs[5:9], refs[9:13], refs[14 : 14 + count]
    attend(group, ordered, blocks, table, o_refs, *refs[14 + count :])


def far_kernel(group, count, *refs):
    q_refs, blocks, refs = refs[:count], refs[count : count + PLANE], refs[count + PLANE :]
    o_refs, table, refs = refs[:count], refs[count : count + 4], refs[count + 4 :]
    ordered, q_ref, shifted_ref, start_vmem, start_smem, sem = refs[:5], *refs[5:10]
    kk_ref, from_ref, meta_ref, norm_ref = table
    slots = (blocks[0].shape[0] - 32) // 2
    copy = start_table(blocks, norm_ref, shifted_ref, start_vmem, start_smem, sem)
    order(group, q_refs, *ordered, q_ref)
    copy.wait()
    finish_table(slots, kk_ref, from_ref, meta_ref, shifted_ref, start_smem)
    attend(group, ordered, blocks, table, o_refs, *refs[10:])


def attend(
    group, ordered, blocks, table, o_refs,
    os_ref, acc_ref, total_ref, top_ref, shift_ref, score_a, score_b, steps_ref,
):
    qs_ref, qcode_ref, back_ref, span_ref, qnorm_ref = ordered
    kk_ref, from_ref, meta_ref, norm_ref = table
    heads = qs_ref.shape[0]
    width = heads * HD
    tokens, padded = back_ref.shape
    each = o_refs[0].shape[0]

    made = jnp.int32(0)
    for r in range(REQS):
        chunk_lo = meta_ref[0, r]
        chunk_hi = meta_ref[1, r]

        def one_group(g, made, r=r, chunk_lo=chunk_lo, chunk_hi=chunk_hi):
            def one_chunk(c, made):
                steps_ref[0, made] = span_ref[0, r] + g * group
                steps_ref[1, made] = c
                steps_ref[2, made] = r * SPAN
                return made + 1

            return lax.fori_loop(chunk_lo, chunk_hi, one_chunk, made)

        made = lax.fori_loop(0, span_ref[1, r], one_group, made)
    for n in range(5):
        steps_ref[0, made + n] = 0
        steps_ref[1, made + n] = 0
        steps_ref[2, made + n] = REQS * SPAN
    acc_ref[...] = jnp.zeros(acc_ref.shape, F32)
    total_ref[...] = jnp.zeros(total_ref.shape, F32)

    large = jnp.max(qnorm_ref[...] * norm_ref[...]) * (1.05 * SCALE2 * SCALE2) > 80.0 * 80.0

    slots = (blocks[0].shape[0] - 32) // 2
    ones = jnp.ones((CHUNK, LANES), BF16)

    def masks(s):
        row0 = pl.multiple_of(steps_ref[0, s], 16)
        first = steps_ref[2, s].astype(F32)
        code = qcode_ref[pl.ds(row0, group), :]
        limit = jnp.where((code >= first) & (code < first + SPAN), code, -1.0)
        row = steps_ref[1, s] * PLANE
        return [kk_ref[pl.ds(row + b, 1), :] <= limit for b in range(PLANE)]

    def slots_of(s, base):
        c = steps_ref[1, s]
        return jnp.concatenate(
            [
                blocks[b][pl.ds(pl.multiple_of(base + from_ref[b, c], 16), LANES), :]
                for b in range(PLANE)
            ],
            axis=0,
        )

    def rows_of(s, h):
        return h, pl.ds(pl.multiple_of(steps_ref[0, s], 16), group), slice(None)

    def scores_of(s):
        q = jnp.concatenate([qs_ref[rows_of(s, h)] for h in range(heads)], axis=0)
        return lax.dot_general(q, slots_of(s, 0), NT, preferred_element_type=F32) * SCALE2

    def weigh(s, scores, shifted):
        seen = [jnp.where(m, 1.0, 0.0).astype(BF16) for m in masks(s)]
        weights = []
        for h in range(heads):
            row = []
            for n in range(PLANE):
                part = scores[h * group : (h + 1) * group, n * LANES : (n + 1) * LANES]
                if shifted:
                    part = jnp.minimum(part - top_ref[rows_of(s, h)], 0.0)
                row.append(jnp.exp2(part).astype(BF16) * seen[n])
            weights.append(jnp.concatenate(row, axis=1))
        out = jnp.dot(
            jnp.concatenate(weights, axis=0),
            jnp.concatenate([slots_of(s, slots), ones], axis=1),
            preferred_element_type=F32,
        )
        for h in range(heads):
            acc_ref[rows_of(s, h)] += out[h * group : (h + 1) * group, :HD]
            total_ref[rows_of(s, h)] += out[h * group : (h + 1) * group, HD:]

    wide = iota((padded, LANES), 1)

    @pl.when(large)
    def _():
        top_ref[...] = jnp.full(top_ref.shape, NEG, F32)

        def look(s, carry):
            scores = scores_of(s)
            seen = masks(s)
            for h in range(heads):
                best = top_ref[rows_of(s, h)]
                for n in range(PLANE):
                    part = scores[h * group : (h + 1) * group, n * LANES : (n + 1) * LANES]
                    best = jnp.maximum(best, jnp.where(seen[n], part, NEG))
                top_ref[rows_of(s, h)] = best
            return carry

        lax.fori_loop(0, made, look, 0)
        block = jnp.zeros((padded, LANES), F32)
        for h in range(heads):
            best = jnp.max(top_ref[h], axis=1, keepdims=True)
            best = jnp.broadcast_to(jnp.where(best < 0.5 * NEG, 0.0, best), top_ref.shape[1:])
            top_ref[h] = best
            block = jnp.where(wide == h, best[:padded], block)
        shift_ref[...] = block

        def step(s, carry):
            weigh(s, scores_of(s), True)
            return carry

        lax.fori_loop(0, made, step, 0)

    @pl.when(jnp.logical_not(large))
    def _():
        shift_ref[...] = jnp.zeros(shift_ref.shape, F32)
        score_a[...] = scores_of(0)

        def four(i, carry):
            for n in range(0, 4, 2):
                score_b[...] = scores_of(4 * i + n + 1)
                weigh(4 * i + n, score_a, False)
                score_a[...] = scores_of(4 * i + n + 2)
                weigh(4 * i + n + 1, score_b, False)
            return carry

        lax.fori_loop(0, (made + 3) // 4, four, 0)

    totals = jnp.zeros((padded, LANES), F32)
    for h in range(heads):
        total = total_ref[h, 0:padded, :]
        totals = jnp.where(wide == h, total, totals)
        scale = 1.0 / jnp.where(total > 0.0, total, 1.0)
        os_ref[:, h * HD : (h + 1) * HD] = (acc_ref[h, 0:padded, :] * scale).astype(BF16)
    some = totals > 0.0
    shares = jnp.where(some, shift_ref[...] + jnp.log2(jnp.where(some, totals, 1.0)), NEG)
    os_ref[:, width:] = three_parts(shares, wide, heads).astype(BF16)
    out = jnp.dot(back_ref[...], os_ref[...], preferred_element_type=F32).astype(BF16)
    for n in range(len(o_refs)):
        o_refs[n][...] = out[n * each : (n + 1) * each, :]


def three_parts(block, wide, heads):
    high = block.astype(BF16).astype(F32)
    middle = (block - high).astype(BF16).astype(F32)
    low = block - high - middle
    out = jnp.where(wide < heads, high, 0.0)
    out = jnp.where((wide >= heads) & (wide < 2 * heads), pltpu.roll(middle, heads, 1), out)
    return jnp.where(
        (wide >= 2 * heads) & (wide < 3 * heads), pltpu.roll(low, 2 * heads, 1), out
    )


def shares_of(ref, heads, rows=slice(None)):
    lab = ref[rows, heads * HD :].astype(F32)
    return lab + pltpu.roll(lab, LANES - heads, 1) + pltpu.roll(lab, LANES - 2 * heads, 1)


def joined(terms, heads):
    shares = [shares_of(ref, heads, rows) for ref, rows in terms]
    best = functools.reduce(jnp.maximum, shares)
    weights = [jnp.exp2(s - best) for s in shares]
    total = sum(weights)
    scale = 1.0 / total
    weights = [w * scale for w in weights]
    outs = []
    for h in range(heads):
        at = slice(h * HD, (h + 1) * HD)
        acc = None
        for w, (ref, rows) in zip(weights, terms):
            term = w[:, h : h + 1] * ref[rows, at].astype(F32)
            acc = term if acc is None else acc + term
        outs.append(acc.astype(BF16))
    return outs, best + jnp.log2(total)


def merge_kernel(up1, down1, up2, down2, from_down, from_up, o_up1, o_down1, o_up2, o_down2):
    tokens = up1.shape[0]
    half = tokens // 2
    heads = (up1.shape[1] - LANES) // HD
    first, second, both = slice(0, half), slice(half, tokens), slice(0, tokens)
    tail = slice(tokens, tokens + half)

    def put(ref, rows, terms):
        outs, share = joined(terms, heads)
        for h in range(heads):
            ref[rows, h * HD : (h + 1) * HD] = outs[h]
        ref[rows, heads * HD :] = three_parts(share, iota(share.shape, 1), heads).astype(BF16)

    put(o_up2, first, [(up2, first), (from_down, tail)])
    o_up2[second, :] = up2[second, :]
    put(o_down2, second, [(down2, second), (from_up, tail)])
    o_down2[first, :] = down2[first, :]
    put(o_up1, both, [(up1, both), (from_down, both)])
    put(o_down1, both, [(down1, both), (from_up, both)])


def combine_kernel(*refs):
    parts, o_ref = refs[:-1], refs[-1]
    heads = o_ref.shape[1] // HD
    outs, _ = joined([(ref, slice(None)) for ref in parts], heads)
    for h in range(heads):
        o_ref[:, h * HD : (h + 1) * HD] = outs[h]


def params(size=VMEM_BYTES):
    return pltpu.CompilerParams(vmem_limit_bytes=size)


def cost(microseconds):
    return pl.CostEstimate(
        flops=int(microseconds * 1.0e9), bytes_accessed=int(microseconds * 3.0e6), transcendentals=0
    )


def on_device(queries, keys, values, key_segment, key_position, query_segment, query_position):
    cycle = lax.axis_size("ctx")
    planes = cycle // PLANE
    tokens, width = queries.shape
    slots = keys.shape[0]
    wide = width + LANES
    kv, qp = pl.pallas_call(
        pack_kernel,
        out_shape=(
            jax.ShapeDtypeStruct((2 * slots + 32, HD), BF16),
            jax.ShapeDtypeStruct((tokens, wide), BF16),
        ),
        in_specs=[pl.BlockSpec(memory_space=pltpu.HBM)] * 7,
        scratch_shapes=[
            pltpu.VMEM((tokens, width), BF16),
            pltpu.VMEM((slots, HD), BF16),
            pltpu.VMEM((slots, HD), BF16),
            pltpu.VMEM((slots // LANES, LANES), jnp.int32),
            pltpu.VMEM((slots // LANES, LANES), jnp.int32),
            pltpu.VMEM((1, tokens), jnp.int32),
            pltpu.VMEM((1, tokens), jnp.int32),
            pltpu.SemaphoreType.DMA((7,)),
        ],
        cost_estimate=cost(3),
        compiler_params=params(ALL_VMEM),
        name="pack",
    )(
        queries, keys, values,
        key_segment.reshape(slots // LANES, LANES), key_position.reshape(slots // LANES, LANES),
        query_segment.reshape(1, tokens), query_position.reshape(1, tokens),
    )

    def swapped(x, bits):
        return lax.ppermute(x, "ctx", [(i, i ^ bits) for i in range(cycle)])

    kv_y = swapped(kv, 2)
    kv_c = swapped(kv, 1)

    def moved(x, steps):
        return lax.ppermute(x, "ctx", [(i, (i + PLANE * steps) % cycle) for i in range(cycle)])

    half = tokens // 2
    up = [qp, moved(qp, 1)]
    down = [qp, moved(qp, -1)]
    up.append(moved(up[1], 1))
    down.append(moved(down[1], -1))
    kv_y, up[2], down[2] = lax.optimization_barrier((kv_y, up[2], down[2]))
    up.append(moved(up[2], 1))
    down.append(moved(down[2], -1))
    kv_yc = swapped(kv_y, 1)
    far = jnp.concatenate([moved(up[3][:half], 1), moved(down[3][half:], -1)], axis=0)

    chunks = (PLANE * slots + PLANE * REQS * 15) // LANES + PLANE * REQS
    smem = pl.BlockSpec(memory_space=pltpu.SMEM)
    vmem = pl.BlockSpec(memory_space=pltpu.VMEM)
    anywhere = pl.BlockSpec(memory_space=pl.ANY)
    blocks = (kv, kv_c, kv_y, kv_yc)
    heads = width // HD
    table_like = (
        jax.ShapeDtypeStruct((chunks * PLANE, LANES), F32),
        jax.ShapeDtypeStruct((PLANE, chunks), jnp.int32),
        jax.ShapeDtypeStruct((2, REQS), jnp.int32),
        jax.ShapeDtypeStruct((8, LANES), F32),
    )
    table_specs = (vmem, smem, smem, vmem)
    ordered_specs = (vmem, vmem, vmem, smem, vmem)
    result = jax.ShapeDtypeStruct((tokens, wide), BF16)

    def ordered_like(count, group):
        padded = count * tokens + REQS * 16
        return (
            jax.ShapeDtypeStruct((heads, padded + group, HD), BF16),
            jax.ShapeDtypeStruct((padded + group, LANES), F32),
            jax.ShapeDtypeStruct((count * tokens, padded), BF16),
            jax.ShapeDtypeStruct((2, REQS), jnp.int32),
            jax.ShapeDtypeStruct((8, LANES), F32),
        )

    def attend_scratch(count, group):
        padded = count * tokens + REQS * 16
        held = (heads, padded + group, LANES)
        most = (count * tokens // group + REQS) * chunks + 5
        return [
            pltpu.VMEM((padded, wide), BF16),
            pltpu.VMEM(held, F32),
            pltpu.VMEM(held, F32),
            pltpu.VMEM(held, F32),
            pltpu.VMEM((padded, LANES), F32),
            pltpu.VMEM((heads * group, CHUNK), F32),
            pltpu.VMEM((heads * group, CHUNK), F32),
            pltpu.SMEM((3, most), jnp.int32),
        ]

    near_blocks = [qp, up[1], down[1], up[2], down[2]]
    far_blocks = [up[3], down[3], far]
    ordered = pl.pallas_call(
        functools.partial(order_kernel, NEAR_GROUP),
        out_shape=ordered_like(5, NEAR_GROUP),
        out_specs=ordered_specs,
        scratch_shapes=[pltpu.VMEM((5 * tokens, wide), BF16)],
        cost_estimate=cost(2),
        compiler_params=params(),
        name="order_near",
    )(*near_blocks)
    in_vmem = [pltpu.VMEM(like.shape, like.dtype) for like in ordered_like(3, FAR_GROUP)]
    in_vmem[3] = pltpu.SMEM((2, REQS), jnp.int32)
    from3, to3, across, *table = pl.pallas_call(
        functools.partial(far_kernel, FAR_GROUP, 3),
        out_shape=(result,) * 3 + table_like,
        in_specs=[vmem] * 7,
        out_specs=(vmem,) * 3 + table_specs,
        scratch_shapes=in_vmem
        + [
            pltpu.VMEM((3 * tokens, wide), BF16),
            pltpu.VMEM((PLANE * 8, slots // LANES, LANES), F32),
            pltpu.VMEM((16, LANES), jnp.int32),
            pltpu.SMEM((16, LANES), jnp.int32),
            pltpu.SemaphoreType.DMA,
        ]
        + attend_scratch(3, FAR_GROUP),
        cost_estimate=cost(8),
        compiler_params=params(),
        name="attend_far",
    )(*far_blocks, *blocks)

    send_down = jnp.concatenate([from3, across[half:]], axis=0)
    send_up = jnp.concatenate([to3, across[:half]], axis=0)
    from_up = moved(send_down, -2)
    from_down = moved(send_up, 2)
    own, below1, above1, below2, above2 = pl.pallas_call(
        functools.partial(near_kernel, NEAR_GROUP, 5),
        out_shape=(result,) * 5,
        in_specs=[*ordered_specs] + [vmem] * PLANE + [*table_specs, anywhere],
        scratch_shapes=attend_scratch(5, NEAR_GROUP),
        cost_estimate=cost(8),
        compiler_params=params(),
        name="attend_near",
    )(*ordered, *blocks, *table, across)
    up1, down1, up2, down2 = pl.pallas_call(
        merge_kernel,
        out_shape=[jax.ShapeDtypeStruct((tokens, wide), BF16)] * 4,
        cost_estimate=cost(2),
        compiler_params=params(),
        name="merge",
    )(above1, below1, above2, below2, from_down, from_up)
    got = [own, moved(up2, 2), moved(down2, -2), moved(up1, 1), moved(down1, -1)]
    return pl.pallas_call(
        combine_kernel,
        out_shape=jax.ShapeDtypeStruct((tokens, width), BF16),
        compiler_params=params(),
        name="combine",
    )(*got)


def solution(mesh):
    placed = (
        P("ctx", "tp"),
        P("ctx", "tp"),
        P("ctx", "tp"),
        P("ctx"),
        P("ctx"),
        P("ctx"),
        P("ctx"),
    )
    return jax.shard_map(
        on_device, mesh=mesh, in_specs=placed, out_specs=P("ctx", "tp"), check_vma=False
    )
```

```python
import functools
import math

import jax
import jax.numpy as jnp
from jax import lax
from jax.experimental import pallas as pl
from jax.experimental.pallas import tpu as pltpu
from jax.sharding import PartitionSpec as P

HD = 128
LANES = 128
REQS = 8
SPAN = 16384
BIG = 1e9
NEG = -1e30
SCALE2 = math.log2(math.e) / math.sqrt(HD)
LN2 = math.log(2.0)
PLANE = 4
CHUNK = PLANE * LANES
NEAR_GROUP = 48
FAR_GROUP = 32
VMEM_BYTES = 32 * 1024 * 1024
ALL_VMEM = 62 * 1024 * 1024
F32 = jnp.float32
BF16 = jnp.bfloat16

NT = (((1,), (1,)), ((), ()))


def iota(shape, dim):
    return lax.broadcasted_iota(jnp.int32, shape, dim)


def pack_kernel(*refs):
    far, (kv_ref, qp_ref), near, sems = refs[:7], refs[7:9], refs[9:16], refs[16]
    copies = [pltpu.make_async_copy(a, b, sems.at[n]) for n, (a, b) in enumerate(zip(far, near))]
    for copy in copies:
        copy.start()
    for copy in copies:
        copy.wait()
    q_ref, k_ref, v_ref, kseg_ref, kpos_ref, qseg_ref, qpos_ref = near
    slots = k_ref.shape[0]
    tiles = slots // LANES
    tokens = q_ref.shape[0]
    width = q_ref.shape[1]

    qseg = qseg_ref[...].astype(F32)
    qhi = (qpos_ref[...] >> 7).astype(F32)
    qlo = (qpos_ref[...] & 127).astype(F32)
    rows = jnp.concatenate([qseg, qhi, qlo, jnp.zeros((LANES - 3, tokens), F32)], axis=0)
    labels = jnp.transpose(rows).astype(BF16)
    qp_ref[:, :width] = q_ref[...]
    qp_ref[:, width:] = labels

    seg = kseg_ref[...]
    pos = kpos_ref[...]
    code = (seg * SPAN + pos).astype(F32)
    ranks = [jnp.zeros((1, LANES), F32) for _ in range(tiles)]
    for t in range(tiles):
        col = jnp.transpose(jnp.broadcast_to(code[t : t + 1, :], (LANES, LANES)))
        for u in range(tiles):
            less = jnp.where(col < code[u : u + 1, :], 1.0, 0.0)
            ranks[u] = ranks[u] + jnp.sum(less, axis=0, keepdims=True)
    rank = jnp.concatenate(ranks, axis=1).astype(jnp.int32)
    place = jnp.where(iota((slots, slots), 0) == rank, 1.0, 0.0).astype(BF16)
    both = jnp.concatenate([k_ref[...], v_ref[...]], axis=1)
    both = jnp.dot(place, both, preferred_element_type=F32).astype(BF16)
    kv_ref[0:slots, :] = both[:, :HD]
    kv_ref[slots : 2 * slots, :] = both[:, HD:]
    flat = lambda x: jnp.concatenate([x[t : t + 1, :] for t in range(tiles)], axis=1)
    labs = jnp.concatenate(
        [flat(seg.astype(F32)), flat((pos >> 7).astype(F32)), flat((pos & 127).astype(F32)),
         jnp.zeros((5, slots), F32)], axis=0)
    moved = lax.dot_general(labs.astype(BF16), place, NT, preferred_element_type=F32)
    parts = [moved[w : w + 1, t * LANES : (t + 1) * LANES] for w in range(3) for t in range(tiles)]
    k = k_ref[...]
    sums = jnp.dot(k * k, jnp.ones((HD, LANES), BF16), preferred_element_type=F32)
    parts.append(jnp.max(sums, axis=0, keepdims=True) * 1.02)
    parts.append(jnp.zeros((31 - 3 * tiles, LANES), F32))
    kv_ref[2 * slots :, :] = jnp.concatenate(parts, axis=0).astype(BF16)


def start_table(blocks, norm_ref, shifted_ref, start_vmem, start_smem, sem):
    slots = (blocks[0].shape[0] - 32) // 2
    tiles = slots // LANES
    lane = iota((tiles, LANES), 1)
    best = jnp.zeros((1, LANES), F32)
    table = jnp.zeros((16, LANES), F32)
    for b in range(PLANE):
        lab = blocks[b][2 * slots : 2 * slots + 32, :].astype(F32)
        code = lab[:tiles] * SPAN + lab[tiles : 2 * tiles] * 128.0 + lab[2 * tiles : 3 * tiles]
        best = jnp.maximum(best, lab[3 * tiles : 3 * tiles + 1])
        below = [
            jnp.sum(jnp.where(code < float(r * SPAN), 1.0, 0.0), axis=0, keepdims=True)
            for r in range(REQS + 1)
        ]
        below.append(jnp.zeros((16 - REQS - 1, LANES), F32))
        counts = jnp.sum(jnp.concatenate(below, axis=0), axis=1, keepdims=True)
        table = jnp.where(iota((16, LANES), 1) == b, counts, table)
    start_vmem[...] = table.astype(jnp.int32)
    copy = pltpu.make_async_copy(start_vmem, start_smem, sem)
    copy.start()
    norm_ref[...] = jnp.broadcast_to(best, norm_ref.shape)
    for b in range(PLANE):
        lab = blocks[b][2 * slots : 2 * slots + 32, :].astype(F32)
        code = lab[:tiles] * SPAN + lab[tiles : 2 * tiles] * 128.0 + lab[2 * tiles : 3 * tiles]
        after = jnp.concatenate([code[1:], code[:1]], axis=0)
        shifted_ref[b * 8] = code
        for n in range(1, 8):
            step = 16 * n
            shifted_ref[b * 8 + n] = jnp.where(
                lane < LANES - step,
                pltpu.roll(code, LANES - step, 1),
                pltpu.roll(after, LANES - step, 1),
            )
    return copy


def finish_table(slots, kk_ref, from_ref, meta_ref, shifted_ref, start_smem):
    lane1 = iota((1, LANES), 1)

    def request(r, made):
        first = (r * SPAN).astype(F32)
        bases = []
        count = jnp.int32(0)
        for b in range(PLANE):
            lo = start_smem[r, b]
            hi = start_smem[r + 1, b]
            base = lo & ~15
            bases.append(base)
            count = jnp.maximum(count, jnp.where(hi > lo, (hi - base + LANES - 1) // LANES, 0))

        def one(j, carry):
            for b in range(PLANE):
                want = bases[b] + j * LANES
                have = jnp.minimum(want, slots - LANES)
                from_ref[b, made + j] = have
                row = shifted_ref[b * 8 + (have % LANES) // 16, pl.ds(have // LANES, 1), :]
                good = (row >= first) & (row < first + SPAN) & (lane1 + have >= want)
                kk_ref[pl.ds((made + j) * PLANE + b, 1), :] = jnp.where(good, row, BIG)
            return carry

        lax.fori_loop(0, count, one, 0)
        meta_ref[0, r] = made
        meta_ref[1, r] = made + count
        return made + count

    lax.fori_loop(0, REQS, request, jnp.int32(0))


def order_kernel(group, *refs):
    order(group, refs[:-6], *refs[-6:])


def order(group, q_refs, qs_ref, qcode_ref, back_ref, span_ref, norm_ref, q_ref):
    each = q_refs[0].shape[0]
    for n, ref in enumerate(q_refs):
        q_ref[n * each : (n + 1) * each, :] = ref[...]
    tokens = q_ref.shape[0]
    heads = qs_ref.shape[0]
    width = heads * HD
    padded = tokens + REQS * 16
    lab = q_ref[:, width:].astype(F32)
    lab_t = jnp.transpose(lab)
    seg_row = lab_t[0:1]
    code_row = seg_row * SPAN + lab_t[1:2] * 128.0 + lab_t[2:3]
    seg_col = lab[:, 0:1]
    code_col = seg_col * SPAN + lab[:, 1:2] * 128.0 + lab[:, 2:3]
    rank_row = jnp.sum(jnp.where(code_col < code_row, 1.0, 0.0), axis=0, keepdims=True)
    rank_col = jnp.sum(jnp.where(code_row < code_col, 1.0, 0.0), axis=1, keepdims=True)
    counts = [
        jnp.sum(jnp.where(seg_row == float(r), 1.0, 0.0), axis=1, keepdims=True) for r in range(REQS)
    ]
    extra = jnp.zeros((1, 1), F32)
    for r in range(REQS):
        rank_row = rank_row + jnp.where(seg_row == float(r), extra, 0.0)
        rank_col = rank_col + jnp.where(seg_col == float(r), extra, 0.0)
        extra = extra + (jnp.ceil(counts[r] * (1.0 / 16.0)) * 16.0 - counts[r])
    used = jnp.int32(0)
    for r in range(REQS):
        count = jnp.max(counts[r]).astype(jnp.int32)
        span_ref[0, r] = used
        span_ref[1, r] = (count + group - 1) // group
        used = used + ((count + 15) // 16) * 16
    place = jnp.where(
        iota((padded, tokens), 0) == rank_row.astype(jnp.int32), 1.0, 0.0
    ).astype(BF16)
    back_ref[...] = jnp.where(
        iota((tokens, padded), 1) == rank_col.astype(jnp.int32), 1.0, 0.0
    ).astype(BF16)
    ones = jnp.ones((HD, LANES), BF16)
    sums = jnp.zeros((padded, LANES), F32)
    for h in range(heads):
        q = jnp.dot(place, q_ref[:, h * HD : (h + 1) * HD], preferred_element_type=F32)
        q = q.astype(BF16)
        qs_ref[h, 0:padded, :] = q
        qs_ref[h, padded:, :] = jnp.zeros((group, HD), BF16)
        sums = jnp.maximum(sums, jnp.dot(q * q, ones, preferred_element_type=F32))
    norm_ref[...] = jnp.broadcast_to(jnp.max(sums, axis=0, keepdims=True), norm_ref.shape)
    lab_s = jnp.dot(place, q_ref[:, width:], preferred_element_type=F32)
    qcode = lab_s[:, 0:1] * SPAN + lab_s[:, 1:2] * 128.0 + lab_s[:, 2:3]
    qcode_ref[0:padded, :] = jnp.broadcast_to(qcode, (padded, LANES))
    qcode_ref[padded:, :] = jnp.zeros((group, LANES), F32)


def near_kernel(group, count, *refs):
    ordered, blocks, table, o_refs = refs[:5], refs[5:9], refs[9:13], refs[14 : 14 + count]
    attend(group, ordered, blocks, table, o_refs, *refs[14 + count :])


def far_kernel(group, count, *refs):
    q_refs, blocks, refs = refs[:count], refs[count : count + PLANE], refs[count + PLANE :]
    o_refs, table, refs = refs[:count], refs[count : count + 4], refs[count + 4 :]
    ordered, q_ref, shifted_ref, start_vmem, start_smem, sem = refs[:5], *refs[5:10]
    kk_ref, from_ref, meta_ref, norm_ref = table
    slots = (blocks[0].shape[0] - 32) // 2
    copy = start_table(blocks, norm_ref, shifted_ref, start_vmem, start_smem, sem)
    order(group, q_refs, *ordered, q_ref)
    copy.wait()
    finish_table(slots, kk_ref, from_ref, meta_ref, shifted_ref, start_smem)
    attend(group, ordered, blocks, table, o_refs, *refs[10:])


def attend(
    group, ordered, blocks, table, o_refs,
    os_ref, acc_ref, total_ref, top_ref, shift_ref, score_a, score_b, steps_ref,
):
    qs_ref, qcode_ref, back_ref, span_ref, qnorm_ref = ordered
    kk_ref, from_ref, meta_ref, norm_ref = table
    heads = qs_ref.shape[0]
    width = heads * HD
    tokens, padded = back_ref.shape
    each = o_refs[0].shape[0]

    made = jnp.int32(0)
    for r in range(REQS):
        chunk_lo = meta_ref[0, r]
        chunk_hi = meta_ref[1, r]

        def one_group(g, made, r=r, chunk_lo=chunk_lo, chunk_hi=chunk_hi):
            def one_chunk(c, made):
                steps_ref[0, made] = span_ref[0, r] + g * group
                steps_ref[1, made] = c
                steps_ref[2, made] = r * SPAN
                return made + 1

            return lax.fori_loop(chunk_lo, chunk_hi, one_chunk, made)

        made = lax.fori_loop(0, span_ref[1, r], one_group, made)
    for n in range(9):
        steps_ref[0, made + n] = 0
        steps_ref[1, made + n] = 0
        steps_ref[2, made + n] = REQS * SPAN
    acc_ref[...] = jnp.zeros(acc_ref.shape, F32)
    total_ref[...] = jnp.zeros(total_ref.shape, F32)

    large = jnp.max(qnorm_ref[...] * norm_ref[...]) * (1.05 * SCALE2 * SCALE2) > 80.0 * 80.0

    slots = (blocks[0].shape[0] - 32) // 2
    ones = jnp.ones((CHUNK, LANES), BF16)

    def masks(s):
        row0 = pl.multiple_of(steps_ref[0, s], 16)
        first = steps_ref[2, s].astype(F32)
        code = qcode_ref[pl.ds(row0, group), :]
        limit = jnp.where((code >= first) & (code < first + SPAN), code, -1.0)
        row = steps_ref[1, s] * PLANE
        return [kk_ref[pl.ds(row + b, 1), :] <= limit for b in range(PLANE)]

    def slots_of(s, base):
        c = steps_ref[1, s]
        return jnp.concatenate(
            [
                blocks[b][pl.ds(pl.multiple_of(base + from_ref[b, c], 16), LANES), :]
                for b in range(PLANE)
            ],
            axis=0,
        )

    def rows_of(s, h):
        return h, pl.ds(pl.multiple_of(steps_ref[0, s], 16), group), slice(None)

    def scores_of(s):
        q = jnp.concatenate([qs_ref[rows_of(s, h)] for h in range(heads)], axis=0)
        return lax.dot_general(q, slots_of(s, 0), NT, preferred_element_type=F32) * SCALE2

    def weigh(s, scores, shifted):
        seen = [jnp.where(m, 1.0, 0.0).astype(BF16) for m in masks(s)]
        weights = []
        for h in range(heads):
            row = []
            for n in range(PLANE):
                part = scores[h * group : (h + 1) * group, n * LANES : (n + 1) * LANES]
                if shifted:
                    part = jnp.minimum(part - top_ref[rows_of(s, h)], 0.0)
                row.append(jnp.exp2(part).astype(BF16) * seen[n])
            weights.append(jnp.concatenate(row, axis=1))
        out = jnp.dot(
            jnp.concatenate(weights, axis=0),
            jnp.concatenate([slots_of(s, slots), ones], axis=1),
            preferred_element_type=F32,
        )
        for h in range(heads):
            acc_ref[rows_of(s, h)] += out[h * group : (h + 1) * group, :HD]
            total_ref[rows_of(s, h)] += out[h * group : (h + 1) * group, HD:]

    wide = iota((padded, LANES), 1)

    @pl.when(large)
    def _():
        top_ref[...] = jnp.full(top_ref.shape, NEG, F32)

        def look(s, carry):
            scores = scores_of(s)
            seen = masks(s)
            for h in range(heads):
                best = top_ref[rows_of(s, h)]
                for n in range(PLANE):
                    part = scores[h * group : (h + 1) * group, n * LANES : (n + 1) * LANES]
                    best = jnp.maximum(best, jnp.where(seen[n], part, NEG))
                top_ref[rows_of(s, h)] = best
            return carry

        lax.fori_loop(0, made, look, 0)
        block = jnp.zeros((padded, LANES), F32)
        for h in range(heads):
            best = jnp.max(top_ref[h], axis=1, keepdims=True)
            best = jnp.broadcast_to(jnp.where(best < 0.5 * NEG, 0.0, best), top_ref.shape[1:])
            top_ref[h] = best
            block = jnp.where(wide == h, best[:padded], block)
        shift_ref[...] = block

        def step(s, carry):
            weigh(s, scores_of(s), True)
            return carry

        lax.fori_loop(0, made, step, 0)

    @pl.when(jnp.logical_not(large))
    def _():
        shift_ref[...] = jnp.zeros(shift_ref.shape, F32)
        score_a[...] = scores_of(0)

        def eight(i, carry):
            for n in range(0, 8, 2):
                score_b[...] = scores_of(8 * i + n + 1)
                weigh(8 * i + n, score_a, False)
                score_a[...] = scores_of(8 * i + n + 2)
                weigh(8 * i + n + 1, score_b, False)
            return carry

        lax.fori_loop(0, (made + 7) // 8, eight, 0)

    totals = jnp.zeros((padded, LANES), F32)
    for h in range(heads):
        total = total_ref[h, 0:padded, :]
        totals = jnp.where(wide == h, total, totals)
        scale = 1.0 / jnp.where(total > 0.0, total, 1.0)
        os_ref[:, h * HD : (h + 1) * HD] = (acc_ref[h, 0:padded, :] * scale).astype(BF16)
    some = totals > 0.0
    shares = jnp.where(some, shift_ref[...] + jnp.log2(jnp.where(some, totals, 1.0)), NEG)
    os_ref[:, width:] = three_parts(shares, wide, heads).astype(BF16)
    out = jnp.dot(back_ref[...], os_ref[...], preferred_element_type=F32).astype(BF16)
    for n in range(len(o_refs)):
        o_refs[n][...] = out[n * each : (n + 1) * each, :]


def three_parts(block, wide, heads):
    high = block.astype(BF16).astype(F32)
    middle = (block - high).astype(BF16).astype(F32)
    low = block - high - middle
    out = jnp.where(wide < heads, high, 0.0)
    out = jnp.where((wide >= heads) & (wide < 2 * heads), pltpu.roll(middle, heads, 1), out)
    return jnp.where(
        (wide >= 2 * heads) & (wide < 3 * heads), pltpu.roll(low, 2 * heads, 1), out
    )


def shares_of(ref, heads, rows=slice(None)):
    lab = ref[rows, heads * HD :].astype(F32)
    return lab + pltpu.roll(lab, LANES - heads, 1) + pltpu.roll(lab, LANES - 2 * heads, 1)


def joined(terms, heads):
    shares = [shares_of(ref, heads, rows) for ref, rows in terms]
    best = functools.reduce(jnp.maximum, shares)
    weights = [jnp.exp2(s - best) for s in shares]
    total = sum(weights)
    scale = 1.0 / total
    weights = [w * scale for w in weights]
    outs = []
    for h in range(heads):
        at = slice(h * HD, (h + 1) * HD)
        acc = None
        for w, (ref, rows) in zip(weights, terms):
            term = w[:, h : h + 1] * ref[rows, at].astype(F32)
            acc = term if acc is None else acc + term
        outs.append(acc.astype(BF16))
    return outs, best + jnp.log2(total)


def merge_kernel(up1, down1, up2, down2, from_down, from_up, o_up1, o_down1, o_up2, o_down2):
    tokens = up1.shape[0]
    half = tokens // 2
    heads = (up1.shape[1] - LANES) // HD
    first, second, both = slice(0, half), slice(half, tokens), slice(0, tokens)
    tail = slice(tokens, tokens + half)

    def put(ref, rows, terms):
        outs, share = joined(terms, heads)
        for h in range(heads):
            ref[rows, h * HD : (h + 1) * HD] = outs[h]
        ref[rows, heads * HD :] = three_parts(share, iota(share.shape, 1), heads).astype(BF16)

    put(o_up2, first, [(up2, first), (from_down, tail)])
    o_up2[second, :] = up2[second, :]
    put(o_down2, second, [(down2, second), (from_up, tail)])
    o_down2[first, :] = down2[first, :]
    put(o_up1, both, [(up1, both), (from_down, both)])
    put(o_down1, both, [(down1, both), (from_up, both)])


def combine_kernel(*refs):
    parts, o_ref = refs[:-1], refs[-1]
    heads = o_ref.shape[1] // HD
    outs, _ = joined([(ref, slice(None)) for ref in parts], heads)
    for h in range(heads):
        o_ref[:, h * HD : (h + 1) * HD] = outs[h]


def params(size=VMEM_BYTES):
    return pltpu.CompilerParams(vmem_limit_bytes=size)


def cost(microseconds):
    return pl.CostEstimate(
        flops=int(microseconds * 1.0e9), bytes_accessed=int(microseconds * 3.0e6), transcendentals=0
    )


def on_device(queries, keys, values, key_segment, key_position, query_segment, query_position):
    cycle = lax.axis_size("ctx")
    planes = cycle // PLANE
    tokens, width = queries.shape
    slots = keys.shape[0]
    wide = width + LANES
    kv, qp = pl.pallas_call(
        pack_kernel,
        out_shape=(
            jax.ShapeDtypeStruct((2 * slots + 32, HD), BF16),
            jax.ShapeDtypeStruct((tokens, wide), BF16),
        ),
        in_specs=[pl.BlockSpec(memory_space=pltpu.HBM)] * 7,
        scratch_shapes=[
            pltpu.VMEM((tokens, width), BF16),
            pltpu.VMEM((slots, HD), BF16),
            pltpu.VMEM((slots, HD), BF16),
            pltpu.VMEM((slots // LANES, LANES), jnp.int32),
            pltpu.VMEM((slots // LANES, LANES), jnp.int32),
            pltpu.VMEM((1, tokens), jnp.int32),
            pltpu.VMEM((1, tokens), jnp.int32),
            pltpu.SemaphoreType.DMA((7,)),
        ],
        cost_estimate=cost(3),
        compiler_params=params(ALL_VMEM),
        name="pack",
    )(
        queries, keys, values,
        key_segment.reshape(slots // LANES, LANES), key_position.reshape(slots // LANES, LANES),
        query_segment.reshape(1, tokens), query_position.reshape(1, tokens),
    )

    def swapped(x, bits):
        return lax.ppermute(x, "ctx", [(i, i ^ bits) for i in range(cycle)])

    kv_y = swapped(kv, 2)
    kv_c = swapped(kv, 1)

    def moved(x, steps):
        return lax.ppermute(x, "ctx", [(i, (i + PLANE * steps) % cycle) for i in range(cycle)])

    half = tokens // 2
    up = [qp, moved(qp, 1)]
    down = [qp, moved(qp, -1)]
    up.append(moved(up[1], 1))
    down.append(moved(down[1], -1))
    kv_y, up[2], down[2] = lax.optimization_barrier((kv_y, up[2], down[2]))
    up.append(moved(up[2], 1))
    down.append(moved(down[2], -1))
    kv_yc = swapped(kv_y, 1)
    far = jnp.concatenate([moved(up[3][:half], 1), moved(down[3][half:], -1)], axis=0)

    chunks = (PLANE * slots + PLANE * REQS * 15) // LANES + PLANE * REQS
    smem = pl.BlockSpec(memory_space=pltpu.SMEM)
    vmem = pl.BlockSpec(memory_space=pltpu.VMEM)
    anywhere = pl.BlockSpec(memory_space=pl.ANY)
    blocks = (kv, kv_c, kv_y, kv_yc)
    heads = width // HD
    table_like = (
        jax.ShapeDtypeStruct((chunks * PLANE, LANES), F32),
        jax.ShapeDtypeStruct((PLANE, chunks), jnp.int32),
        jax.ShapeDtypeStruct((2, REQS), jnp.int32),
        jax.ShapeDtypeStruct((8, LANES), F32),
    )
    table_specs = (vmem, smem, smem, vmem)
    ordered_specs = (vmem, vmem, vmem, smem, vmem)
    result = jax.ShapeDtypeStruct((tokens, wide), BF16)

    def ordered_like(count, group):
        padded = count * tokens + REQS * 16
        return (
            jax.ShapeDtypeStruct((heads, padded + group, HD), BF16),
            jax.ShapeDtypeStruct((padded + group, LANES), F32),
            jax.ShapeDtypeStruct((count * tokens, padded), BF16),
            jax.ShapeDtypeStruct((2, REQS), jnp.int32),
            jax.ShapeDtypeStruct((8, LANES), F32),
        )

    def attend_scratch(count, group):
        padded = count * tokens + REQS * 16
        held = (heads, padded + group, LANES)
        most = (count * tokens // group + REQS) * chunks + 9
        return [
            pltpu.VMEM((padded, wide), BF16),
            pltpu.VMEM(held, F32),
            pltpu.VMEM(held, F32),
            pltpu.VMEM(held, F32),
            pltpu.VMEM((padded, LANES), F32),
            pltpu.VMEM((heads * group, CHUNK), F32),
            pltpu.VMEM((heads * group, CHUNK), F32),
            pltpu.SMEM((3, most), jnp.int32),
        ]

    near_blocks = [qp, up[1], down[1], up[2], down[2]]
    far_blocks = [up[3], down[3], far]
    ordered = pl.pallas_call(
        functools.partial(order_kernel, NEAR_GROUP),
        out_shape=ordered_like(5, NEAR_GROUP),
        out_specs=ordered_specs,
        scratch_shapes=[pltpu.VMEM((5 * tokens, wide), BF16)],
        cost_estimate=cost(2),
        compiler_params=params(),
        name="order_near",
    )(*near_blocks)
    in_vmem = [pltpu.VMEM(like.shape, like.dtype) for like in ordered_like(3, FAR_GROUP)]
    in_vmem[3] = pltpu.SMEM((2, REQS), jnp.int32)
    from3, to3, across, *table = pl.pallas_call(
        functools.partial(far_kernel, FAR_GROUP, 3),
        out_shape=(result,) * 3 + table_like,
        in_specs=[vmem] * 7,
        out_specs=(vmem,) * 3 + table_specs,
        scratch_shapes=in_vmem
        + [
            pltpu.VMEM((3 * tokens, wide), BF16),
            pltpu.VMEM((PLANE * 8, slots // LANES, LANES), F32),
            pltpu.VMEM((16, LANES), jnp.int32),
            pltpu.SMEM((16, LANES), jnp.int32),
            pltpu.SemaphoreType.DMA,
        ]
        + attend_scratch(3, FAR_GROUP),
        cost_estimate=cost(8),
        compiler_params=params(),
        name="attend_far",
    )(*far_blocks, *blocks)

    send_down = jnp.concatenate([from3, across[half:]], axis=0)
    send_up = jnp.concatenate([to3, across[:half]], axis=0)
    from_up = moved(send_down, -2)
    from_down = moved(send_up, 2)
    own, below1, above1, below2, above2 = pl.pallas_call(
        functools.partial(near_kernel, NEAR_GROUP, 5),
        out_shape=(result,) * 5,
        in_specs=[*ordered_specs] + [vmem] * PLANE + [*table_specs, anywhere],
        scratch_shapes=attend_scratch(5, NEAR_GROUP),
        cost_estimate=cost(8),
        compiler_params=params(),
        name="attend_near",
    )(*ordered, *blocks, *table, across)
    up1, down1, up2, down2 = pl.pallas_call(
        merge_kernel,
        out_shape=[jax.ShapeDtypeStruct((tokens, wide), BF16)] * 4,
        cost_estimate=cost(2),
        compiler_params=params(),
        name="merge",
    )(above1, below1, above2, below2, from_down, from_up)
    got = [own, moved(up2, 2), moved(down2, -2), moved(up1, 1), moved(down1, -1)]
    return pl.pallas_call(
        combine_kernel,
        out_shape=jax.ShapeDtypeStruct((tokens, width), BF16),
        compiler_params=params(),
        name="combine",
    )(*got)


def solution(mesh):
    placed = (
        P("ctx", "tp"),
        P("ctx", "tp"),
        P("ctx", "tp"),
        P("ctx"),
        P("ctx"),
        P("ctx"),
        P("ctx"),
    )
    return jax.shard_map(
        on_device, mesh=mesh, in_specs=placed, out_specs=P("ctx", "tp"), check_vma=False
    )
```
